32 devices in a mesh: row: 8 (over z, y), col: 4 (over x, core).
Axes of the slice: x: 2, y: 2, z: 4, core: 2. Of those that a mesh axis runs over, the one named last changes fastest.
Arguments:
- embeddings: bfloat16 [1024, 768], P(('row', 'col')), may hold values from -8 to 8
- start_block: float32 [64, 1024], P(None, ('row', 'col')), may hold values from -6 to 6
Outputs:
- spectral_block: float32 [64, 1024], P(None, ('row', 'col'))
The draws below stay inside these ranges and needn't reach their ends.
All inputs are finite; a program needn't handle non-finite values.
Results may differ from the reference program's by a relative error of at most 0.0059.
Values may be sent and summed in bfloat16 or wider, within the bound.
No kernel may reach another device: no remote copies, remote signals or barrier semaphores. Data moves between devices by JAX's collectives and lax.ppermute only.
A program may use at most 64 MiB of HBM per device.

```python
import math
import jax
import jax.numpy as jnp
from jax import lax

D = 768
VECS = 64
ITERS = 4
PT_DEV = 32
POINTS = 1024
N_ROW = 8
N_COL = 4


def draw_embeddings(key, part):
    key = jax.random.fold_in(key, 11)
    key_centre, key_label, key_noise = jax.random.split(key, 3)
    labels = jax.random.randint(key_label, (POINTS,), 0, 128)
    centres = jax.random.normal(key_centre, (128, D), jnp.float32)
    noise = 0.5 * jax.random.normal(key_noise, (POINTS, D), jnp.float32)
    values = jnp.clip(centres[labels] + noise, -8.0, 8.0)
    return values.astype(jnp.bfloat16)


def levels(rng, extent, shards, smallest, largest):
    factor_of, own = 1.0, jax.random.fold_in(rng, 6)
    for axis_at, blocks in shards:
        heights = jnp.exp(jax.random.uniform(jax.random.fold_in(own, axis_at), (blocks,), jnp.float32, smallest / len(shards), largest / len(shards)))
        factor_of = factor_of * jnp.repeat(heights, extent[axis_at] // blocks).reshape([-1 if axis == axis_at else 1 for axis in range(len(extent))])
    return factor_of


def bell_draw(key, extent, width, reach, cuts=(), dtype=jnp.bfloat16):
    loudness = levels(key, extent, cuts, -0.22, 0.18) if cuts else 1.0
    array = jax.random.normal(key, extent, jnp.float32) * width * loudness
    return jnp.minimum(jnp.maximum(array, -reach), reach).astype(dtype)


def setup_inputs(seed: int = 0) -> dict:
    arg_keys = jax.random.split(jax.random.key(seed), 3)
    return {
        "embeddings": draw_embeddings(jax.random.fold_in(arg_keys[2], 71), 0),
        "start_block": bell_draw(arg_keys[1], (VECS, POINTS), 1.0, 6.0, ((1, 32),), jnp.float32),
    }


TEMPER = 0.5

def kernel_rows(left, left_sq, right, right_sq):
    inner = jnp.dot(left.astype(jnp.float32), right.T.astype(jnp.float32), preferred_element_type=jnp.float32)
    return jnp.exp(-(left_sq[:, None] + right_sq[None, :] - 2.0 * inner) / (TEMPER * left.shape[1]))

def reference(embeddings, start_block):
    block = N_COL * PT_DEV
    count = N_ROW
    squares = lax.optimization_barrier(jnp.sum(jnp.square(embeddings.astype(jnp.float32)), axis=1))
    pieces = embeddings.reshape(count, block, D)
    square_pieces = squares.reshape(count, block)

    def degree_piece(args):
        left, left_sq = args
        return lax.optimization_barrier(jnp.sum(kernel_rows(left, left_sq, embeddings, squares), axis=1))
    degree = lax.map(degree_piece, (pieces, square_pieces)).reshape(POINTS)
    scale = 1.0 / jnp.sqrt(degree)
    vectors = start_block
    for sweep in range(ITERS):
        scaled = (vectors * scale[None, :]).astype(jnp.bfloat16)

        def product_piece(args):
            left, left_sq = args
            tile = kernel_rows(left, left_sq, embeddings, squares).astype(jnp.bfloat16)
            return jnp.dot(scaled.astype(jnp.float32), tile.T.astype(jnp.float32), preferred_element_type=jnp.float32)
        partial_rows = lax.map(product_piece, (pieces, square_pieces))
        mixed = jnp.transpose(partial_rows, (1, 0, 2)).reshape(VECS, POINTS) * scale[None, :]
        gram = jnp.dot(mixed, mixed.T, precision=lax.Precision.HIGHEST)
        factor = jnp.linalg.cholesky(gram)
        vectors = jax.scipy.linalg.solve_triangular(factor, mixed, lower=True)
    return vectors * math.sqrt(POINTS)
```

```python
import functools
import math

import jax
import jax.numpy as jnp
from jax import lax
from jax.experimental import pallas as pl
from jax.experimental.pallas import tpu as pltpu
from jax.sharding import PartitionSpec as P

ITERS = 4
TEMPER = 0.5
HIGHEST = lax.Precision.HIGHEST
NT = (((1,), (1,)), ((), ()))
NN = (((1,), (0,)), ((), ()))


def lane_splat(x, c):
    return jnp.broadcast_to(x[:, c : c + 1], x.shape)


def row_splat(x, r):
    return jnp.broadcast_to(x[r : r + 1, :], x.shape)


def reciprocal(p):
    q = pltpu.reciprocal(p, approx=True)
    q = q * (2.0 - p * q)
    return q * (2.0 - p * q)


def inverse_factor(tiles):
    count = len(tiles)
    sub = lax.broadcasted_iota(jnp.int32, tiles[0].shape, 0)
    pivots = [None] * count
    for b in range(count):
        columns = [[lane_splat(tiles[t], 8 * b + j) for t in range(b, count)] for j in range(8)]
        factors, rows = [], []
        for j in range(8):
            pivot = row_splat(columns[j][0], j)
            q = reciprocal(pivot)
            m = [d * q for d in columns[j]]
            m[0] = jnp.where(sub > j, m[0], 0.0)
            row = row_splat(tiles[b], j)
            tiles[b] = tiles[b] - m[0] * row
            pivots[b] = pivot if j == 0 else jnp.where(sub >= j, pivot, pivots[b])
            for l in range(j + 1, 8):
                head = row_splat(columns[l][0], j)
                columns[l] = [d - f * head for d, f in zip(columns[l], m)]
            factors.append(m)
            rows.append(row)
        for t in range(b + 1, count):
            total = factors[0][t - b] * rows[0]
            for j in range(1, 8):
                total = total + factors[j][t - b] * rows[j]
            tiles[t] = tiles[t] - total
    return [tile * lax.rsqrt(p) for tile, p in zip(tiles, pivots)]


def embed_kernel(pieces, own, vecs, feat, *refs):
    piece_refs, out_ref = refs[:pieces], refs[pieces]
    e_ref, k_ref, v_ref, m_ref = refs[pieces + 1 :]
    per = piece_refs[0].shape[0]
    points = pieces * per
    for i, piece in enumerate(piece_refs):
        e_ref[i * per : (i + 1) * per, :] = piece[:, :feat]
        x0 = piece[:, feat : feat + vecs].astype(jnp.float32) + piece[:, feat + vecs : feat + 2 * vecs].astype(jnp.float32)
        v_ref[:, i * per : (i + 1) * per] = x0.T
    eye = lax.broadcasted_iota(jnp.int32, (per, per), 0) == lax.broadcasted_iota(jnp.int32, (per, per), 1)
    cols, rows = [], []
    for i in range(pieces):
        e = e_ref[i * per : (i + 1) * per, :]
        d = jnp.where(eye, lax.dot_general(e, e, NT, preferred_element_type=jnp.float32), 0.0)
        cols.append(jnp.sum(d, axis=1, keepdims=True))
        rows.append(jnp.sum(d, axis=0, keepdims=True))
    row_sq = jnp.concatenate(rows, axis=1)
    rate = 1.0 / (TEMPER * feat)
    degree = jnp.zeros((1, points), jnp.float32)
    step = 2 * per
    for i in range(points // step):
        g = lax.dot_general(e_ref[i * step : (i + 1) * step, :], e_ref[...], NT, preferred_element_type=jnp.float32)
        col_sq = jnp.concatenate(cols[2 * i : 2 * i + 2], axis=0)
        k = jnp.exp((2.0 * g - col_sq - row_sq) * rate)
        degree = degree + jnp.sum(k, axis=0, keepdims=True)
        k_ref[i * step : (i + 1) * step, :] = k.astype(jnp.bfloat16)
    scale = 1.0 / jnp.sqrt(degree)
    lane = lax.broadcasted_iota(jnp.int32, (vecs, 2 * vecs), 1)
    unit = (lane == lax.broadcasted_iota(jnp.int32, (vecs, 2 * vecs), 0) + vecs).astype(jnp.float32)
    for sweep in range(ITERS):
        scaled = (v_ref[...] * scale).astype(jnp.bfloat16)
        mixed = lax.dot_general(scaled, k_ref[...], NN, preferred_element_type=jnp.float32) * scale
        m_ref[:vecs, :] = mixed
        m_ref[vecs:, :] = mixed
        gram = lax.dot_general(mixed, m_ref[...], NT, preferred_element_type=jnp.float32, precision=HIGHEST)
        full = jnp.where(lane < vecs, gram, unit)
        inv = jnp.concatenate(inverse_factor([full[8 * t : 8 * t + 8, :] for t in range(vecs // 8)]), axis=0)
        inv = jnp.where(lane < vecs, 0.0, inv)
        if sweep < ITERS - 1:
            v_ref[...] = lax.dot_general(inv, m_ref[...], NN, preferred_element_type=jnp.float32, precision=HIGHEST)
        else:
            last = lax.dot_general(inv, m_ref[:, :per], NN, preferred_element_type=jnp.float32, precision=HIGHEST)
            out_ref[...] = last.T[:own, :] * math.sqrt(points)


def exchange(x, rows, cols, partner):
    pairs = []
    for r in range(rows):
        for c in range(cols):
            r2, c2 = partner(r, c)
            pairs.append((r * cols + c, r2 * cols + c2))
    return lax.ppermute(x, ("row", "col"), pairs)


def replicated(embeddings, start_block, rows, cols):
    own, feat = embeddings.shape
    vecs = start_block.shape[0]
    send = functools.partial(exchange, rows=rows, cols=cols)
    start = start_block.T
    high = start.astype(jnp.bfloat16)
    low = (start - high.astype(jnp.float32)).astype(jnp.bfloat16)
    mine = jnp.concatenate([embeddings, high, low], axis=1)
    along_z = [send(mine, partner=lambda r, c, d=d: (r ^ (2 * d), c)) for d in (1, 2, 3)]
    a = jnp.concatenate([mine] + along_z, axis=0)
    b = send(a, partner=lambda r, c: (r, c ^ 2) if c & 1 else (r ^ 1, c))
    c_ = send(a, partner=lambda r, c: (r ^ 1, c) if c & 1 else (r, c ^ 2))
    d_ = send(b, partner=lambda r, c: (r ^ 1, c) if c & 1 else (r, c ^ 2))
    pieces = []
    for piece in (a, b, c_, d_):
        pieces += [piece, send(piece, partner=lambda r, c: (r, c ^ 1))]
    count, per = len(pieces), a.shape[0]
    points = count * per
    return pl.pallas_call(
        functools.partial(embed_kernel, count, own, vecs, feat),
        out_shape=jax.ShapeDtypeStruct((own, vecs), jnp.float32),
        in_specs=[pl.BlockSpec(memory_space=pltpu.VMEM)] * count,
        out_specs=pl.BlockSpec(memory_space=pltpu.VMEM),
        scratch_shapes=[
            pltpu.VMEM((points, feat), jnp.bfloat16),
            pltpu.VMEM((points, points), jnp.bfloat16),
            pltpu.VMEM((vecs, points), jnp.float32),
            pltpu.VMEM((2 * vecs, points), jnp.float32),
        ],
        compiler_params=pltpu.CompilerParams(vmem_limit_bytes=40 * 1024 * 1024),
    )(*pieces).T


def kernel_block(left, left_sq, right):
    right_sq = jnp.sum(jnp.square(right.astype(jnp.float32)), axis=1)
    inner = lax.dot_general(left, right, NT, preferred_element_type=jnp.float32)
    return jnp.exp(-(left_sq[:, None] + right_sq[None, :] - 2.0 * inner) / (TEMPER * left.shape[1]))


def distributed(embeddings, start_block):
    per_device = embeddings.shape[0]
    total = lax.axis_size("row") * lax.axis_size("col") * per_device
    row_block = lax.all_gather(embeddings, "col", axis=0, tiled=True)
    row_sq = jnp.sum(jnp.square(row_block.astype(jnp.float32)), axis=1)
    vectors = start_block
    column_block = lax.all_gather(embeddings, "row", axis=0, tiled=True)
    degree_terms = jnp.sum(kernel_block(row_block, row_sq, column_block), axis=1)
    degree = lax.psum_scatter(degree_terms, "col", scatter_dimension=0, tiled=True)
    scale = 1.0 / jnp.sqrt(degree)
    for sweep in range(ITERS):
        scaled = (vectors * scale[None, :]).astype(jnp.bfloat16)
        column_vectors = lax.all_gather(scaled, "row", axis=1, tiled=True)
        tile = kernel_block(row_block, row_sq, column_block).astype(jnp.bfloat16)
        partial_rows = lax.dot_general(column_vectors, tile, NT, preferred_element_type=jnp.float32)
        mixed = lax.psum_scatter(partial_rows, "col", scatter_dimension=1, tiled=True) * scale[None, :]
        gram = lax.psum(jnp.dot(mixed, mixed.T, precision=HIGHEST), ("row", "col"))
        factor = jnp.linalg.cholesky(gram)
        vectors = jax.scipy.linalg.solve_triangular(factor, mixed, lower=True)
    return vectors * math.sqrt(total)


def solution(mesh):
    rows, cols = mesh.shape["row"], mesh.shape["col"]

    def body(embeddings, start_block):
        if (rows, cols) == (8, 4) and embeddings.shape[0] * 4 == 128 and start_block.shape[0] == 64:
            return replicated(embeddings, start_block, rows, cols)
        return distributed(embeddings, start_block)

    return jax.shard_map(
        body,
        mesh=mesh,
        in_specs=(P(("row", "col"), None), P(None, ("row", "col"))),
        out_specs=P(None, ("row", "col")),
        check_vma=False,
    )
```

```python
import functools
import math

import jax
import jax.numpy as jnp
from jax import lax
from jax.experimental import pallas as pl
from jax.experimental.pallas import tpu as pltpu
from jax.sharding import PartitionSpec as P

ITERS = 4
TEMPER = 0.5
HIGHEST = lax.Precision.HIGHEST
NT = (((1,), (1,)), ((), ()))
NN = (((1,), (0,)), ((), ()))


def lane_splat(x, c):
    return jnp.broadcast_to(x[:, c : c + 1], x.shape)


def row_splat(x, r):
    return jnp.broadcast_to(x[r : r + 1, :], x.shape)


def reciprocal(p):
    q = pltpu.reciprocal(p, approx=True)
    q = q * (2.0 - p * q)
    return q * (2.0 - p * q)


def inverse_factor(tiles):
    count = len(tiles)
    sub = lax.broadcasted_iota(jnp.int32, tiles[0].shape, 0)
    pivots = [None] * count
    for b in range(count):
        columns = [[lane_splat(tiles[t], 8 * b + j) for t in range(b, count)] for j in range(8)]
        factors, rows = [], []
        for j in range(8):
            pivot = row_splat(columns[j][0], j)
            q = reciprocal(pivot)
            m = [d * q for d in columns[j]]
            m[0] = jnp.where(sub > j, m[0], 0.0)
            row = row_splat(tiles[b], j)
            tiles[b] = tiles[b] - m[0] * row
            pivots[b] = pivot if j == 0 else jnp.where(sub >= j, pivot, pivots[b])
            for l in range(j + 1, 8):
                head = row_splat(columns[l][0], j)
                columns[l] = [d - f * head for d, f in zip(columns[l], m)]
            factors.append(m)
            rows.append(row)
        for t in range(b + 1, count):
            total = factors[0][t - b] * rows[0]
            for j in range(1, 8):
                total = total + factors[j][t - b] * rows[j]
            tiles[t] = tiles[t] - total
    return [tile * lax.rsqrt(p) for tile, p in zip(tiles, pivots)]


def pack_kernel(vecs, feat, e_ref, s_ref, o_ref):
    o_ref[:, :feat] = e_ref[...]
    high = s_ref[...].astype(jnp.bfloat16)
    low = (s_ref[...] - high.astype(jnp.float32)).astype(jnp.bfloat16)
    o_ref[:, feat:] = jnp.concatenate([high, low], axis=1)


def embed_kernel(pieces, own, vecs, feat, *refs):
    piece_refs, out_ref = refs[:pieces], refs[pieces]
    e_ref, k_ref, v_ref, m_ref = refs[pieces + 1 :]
    per = piece_refs[0].shape[0]
    points = pieces * per
    for i, piece in enumerate(piece_refs):
        e_ref[i * per : (i + 1) * per, :] = piece[:, :feat]
        x0 = piece[:, feat : feat + vecs].astype(jnp.float32) + piece[:, feat + vecs : feat + 2 * vecs].astype(jnp.float32)
        v_ref[:, i * per : (i + 1) * per] = x0.T
    eye = lax.broadcasted_iota(jnp.int32, (per, per), 0) == lax.broadcasted_iota(jnp.int32, (per, per), 1)
    cols, rows = [], []
    for i in range(pieces):
        e = e_ref[i * per : (i + 1) * per, :]
        d = jnp.where(eye, lax.dot_general(e, e, NT, preferred_element_type=jnp.float32), 0.0)
        cols.append(jnp.sum(d, axis=1, keepdims=True))
        rows.append(jnp.sum(d, axis=0, keepdims=True))
    row_sq = jnp.concatenate(rows, axis=1)
    rate = 1.0 / (TEMPER * feat)
    degree = jnp.zeros((1, points), jnp.float32)
    step = 2 * per
    for i in range(points // step):
        g = lax.dot_general(e_ref[i * step : (i + 1) * step, :], e_ref[...], NT, preferred_element_type=jnp.float32)
        col_sq = jnp.concatenate(cols[2 * i : 2 * i + 2], axis=0)
        k = jnp.exp((2.0 * g - col_sq - row_sq) * rate)
        degree = degree + jnp.sum(k, axis=0, keepdims=True)
        k_ref[i * step : (i + 1) * step, :] = k.astype(jnp.bfloat16)
    scale = 1.0 / jnp.sqrt(degree)
    lane = lax.broadcasted_iota(jnp.int32, (vecs, 2 * vecs), 1)
    unit = (lane == lax.broadcasted_iota(jnp.int32, (vecs, 2 * vecs), 0) + vecs).astype(jnp.float32)
    for sweep in range(ITERS):
        scaled = (v_ref[...] * scale).astype(jnp.bfloat16)
        mixed = lax.dot_general(scaled, k_ref[...], NN, preferred_element_type=jnp.float32) * scale
        m_ref[:vecs, :] = mixed
        m_ref[vecs:, :] = mixed
        gram = lax.dot_general(mixed, m_ref[...], NT, preferred_element_type=jnp.float32, precision=HIGHEST)
        full = jnp.where(lane < vecs, gram, unit)
        inv = jnp.concatenate(inverse_factor([full[8 * t : 8 * t + 8, :] for t in range(vecs // 8)]), axis=0)
        inv = jnp.where(lane < vecs, 0.0, inv)
        if sweep < ITERS - 1:
            v_ref[...] = lax.dot_general(inv, m_ref[...], NN, preferred_element_type=jnp.float32, precision=HIGHEST)
        else:
            last = lax.dot_general(inv, m_ref[:, :per], NN, preferred_element_type=jnp.float32, precision=HIGHEST)
            out_ref[...] = last.T[:own, :] * math.sqrt(points)


def exchange(x, rows, cols, partner):
    pairs = []
    for r in range(rows):
        for c in range(cols):
            r2, c2 = partner(r, c)
            pairs.append((r * cols + c, r2 * cols + c2))
    return lax.ppermute(x, ("row", "col"), pairs)


def replicated(embeddings, start_block, rows, cols):
    own, feat = embeddings.shape
    vecs = start_block.shape[0]
    send = functools.partial(exchange, rows=rows, cols=cols)
    mine = pl.pallas_call(
        functools.partial(pack_kernel, vecs, feat),
        out_shape=jax.ShapeDtypeStruct((own, feat + 2 * vecs), jnp.bfloat16),
        in_specs=[pl.BlockSpec(memory_space=pltpu.VMEM)] * 2,
        out_specs=pl.BlockSpec(memory_space=pltpu.VMEM),
    )(embeddings, start_block.T)
    along_z = [send(mine, partner=lambda r, c, d=d: (r ^ (2 * d), c)) for d in (1, 2, 3)]
    a = jnp.concatenate([mine] + along_z, axis=0)
    b = send(a, partner=lambda r, c: (r, c ^ 2) if c & 1 else (r ^ 1, c))
    c_ = send(a, partner=lambda r, c: (r ^ 1, c) if c & 1 else (r, c ^ 2))
    d_ = send(b, partner=lambda r, c: (r ^ 1, c) if c & 1 else (r, c ^ 2))
    pieces = []
    for piece in (a, b, c_, d_):
        pieces += [piece, send(piece, partner=lambda r, c: (r, c ^ 1))]
    count, per = len(pieces), a.shape[0]
    points = count * per
    return pl.pallas_call(
        functools.partial(embed_kernel, count, own, vecs, feat),
        out_shape=jax.ShapeDtypeStruct((own, vecs), jnp.float32),
        in_specs=[pl.BlockSpec(memory_space=pltpu.VMEM)] * count,
        out_specs=pl.BlockSpec(memory_space=pltpu.VMEM),
        scratch_shapes=[
            pltpu.VMEM((points, feat), jnp.bfloat16),
            pltpu.VMEM((points, points), jnp.bfloat16),
            pltpu.VMEM((vecs, points), jnp.float32),
            pltpu.VMEM((2 * vecs, points), jnp.float32),
        ],
        compiler_params=pltpu.CompilerParams(vmem_limit_bytes=40 * 1024 * 1024),
    )(*pieces).T


def kernel_block(left, left_sq, right):
    right_sq = jnp.sum(jnp.square(right.astype(jnp.float32)), axis=1)
    inner = lax.dot_general(left, right, NT, preferred_element_type=jnp.float32)
    return jnp.exp(-(left_sq[:, None] + right_sq[None, :] - 2.0 * inner) / (TEMPER * left.shape[1]))


def distributed(embeddings, start_block):
    per_device = embeddings.shape[0]
    total = lax.axis_size("row") * lax.axis_size("col") * per_device
    row_block = lax.all_gather(embeddings, "col", axis=0, tiled=True)
    row_sq = jnp.sum(jnp.square(row_block.astype(jnp.float32)), axis=1)
    vectors = start_block
    column_block = lax.all_gather(embeddings, "row", axis=0, tiled=True)
    degree_terms = jnp.sum(kernel_block(row_block, row_sq, column_block), axis=1)
    degree = lax.psum_scatter(degree_terms, "col", scatter_dimension=0, tiled=True)
    scale = 1.0 / jnp.sqrt(degree)
    for sweep in range(ITERS):
        scaled = (vectors * scale[None, :]).astype(jnp.bfloat16)
        column_vectors = lax.all_gather(scaled, "row", axis=1, tiled=True)
        tile = kernel_block(row_block, row_sq, column_block).astype(jnp.bfloat16)
        partial_rows = lax.dot_general(column_vectors, tile, NT, preferred_element_type=jnp.float32)
        mixed = lax.psum_scatter(partial_rows, "col", scatter_dimension=1, tiled=True) * scale[None, :]
        gram = lax.psum(jnp.dot(mixed, mixed.T, precision=HIGHEST), ("row", "col"))
        factor = jnp.linalg.cholesky(gram)
        vectors = jax.scipy.linalg.solve_triangular(factor, mixed, lower=True)
    return vectors * math.sqrt(total)


def solution(mesh):
    rows, cols = mesh.shape["row"], mesh.shape["col"]

    def body(embeddings, start_block):
        if (rows, cols) == (8, 4) and embeddings.shape[0] * 4 == 128 and start_block.shape[0] == 64:
            return replicated(embeddings, start_block, rows, cols)
        return distributed(embeddings, start_block)

    return jax.shard_map(
        body,
        mesh=mesh,
        in_specs=(P(("row", "col"), None), P(None, ("row", "col"))),
        out_specs=P(None, ("row", "col")),
        check_vma=False,
    )
```

```python
import functools
import math

import jax
import jax.numpy as jnp
from jax import lax
from jax.experimental import pallas as pl
from jax.experimental.pallas import tpu as pltpu
from jax.sharding import PartitionSpec as P

ITERS = 4
TEMPER = 0.5
HIGHEST = lax.Precision.HIGHEST
NT = (((1,), (1,)), ((), ()))
NN = (((1,), (0,)), ((), ()))


def lane_splat(x, c):
    return jnp.broadcast_to(x[:, c : c + 1], x.shape)


def row_splat(x, r):
    return jnp.broadcast_to(x[r : r + 1, :], x.shape)


def inverse_factor(tiles):
    count = len(tiles)
    sub = lax.broadcasted_iota(jnp.int32, tiles[0].shape, 0)
    pivots = [None] * count
    ahead = [lane_splat(tiles[0], j) for j in range(8)]
    for b in range(count):
        columns = [[ahead[j]] + [lane_splat(tiles[t], 8 * b + j) for t in range(b + 1, count)] for j in range(8)]
        if b + 1 < count:
            ahead = [lane_splat(tiles[b + 1], 8 * (b + 1) + j) for j in range(8)]
        factors, rows = [], []
        for j in range(8):
            pivot = row_splat(columns[j][0], j)
            q = pltpu.reciprocal(pivot, approx=True)
            m = [d * q for d in columns[j]]
            for l in range(j + 1, 8):
                head = row_splat(columns[l][0], j)
                columns[l] = [d - f * head for d, f in zip(columns[l], m)]
            if b + 1 < count:
                ahead = [d - m[1] * row_splat(columns[j][1], l) for l, d in enumerate(ahead)]
            row = row_splat(tiles[b], j)
            tiles[b] = tiles[b] - jnp.where(sub > j, m[0], 0.0) * row
            pivots[b] = pivot if j == 0 else jnp.where(sub >= j, pivot, pivots[b])
            factors.append(m)
            rows.append(row)
        for t in range(b + 1, count):
            total = factors[0][t - b] * rows[0]
            for j in range(1, 8):
                total = total + factors[j][t - b] * rows[j]
            tiles[t] = tiles[t] - total
    return [tile * lax.rsqrt(p) for tile, p in zip(tiles, pivots)]


def pack_kernel(vecs, feat, e_ref, s_ref, o_ref):
    o_ref[:, :feat] = e_ref[...]
    high = s_ref[...].astype(jnp.bfloat16)
    low = (s_ref[...] - high.astype(jnp.float32)).astype(jnp.bfloat16)
    o_ref[:, feat:] = jnp.concatenate([high, low], axis=1)


def split(x, parts):
    out = []
    for _ in range(parts - 1):
        out.append(x.astype(jnp.bfloat16))
        x = x - out[-1].astype(jnp.float32)
    return out + [x.astype(jnp.bfloat16)]


def dot(a, b, dims=NN):
    return lax.dot_general(a, b, dims, preferred_element_type=jnp.float32)


def embed_kernel(pieces, own, vecs, feat, *refs):
    piece_refs, out_ref = refs[:pieces], refs[pieces]
    e_ref, k_ref, v_ref, m_ref = refs[pieces + 1 :]
    per = piece_refs[0].shape[0]
    points = pieces * per
    for i, piece in enumerate(piece_refs):
        e_ref[i * per : (i + 1) * per, :] = piece[:, :feat]
        x0 = piece[:, feat : feat + vecs].astype(jnp.float32) + piece[:, feat + vecs : feat + 2 * vecs].astype(jnp.float32)
        v_ref[:, i * per : (i + 1) * per] = x0.T
    eye = lax.broadcasted_iota(jnp.int32, (per, per), 0) == lax.broadcasted_iota(jnp.int32, (per, per), 1)
    cols, rows = [], []
    for i in range(pieces):
        e = e_ref[i * per : (i + 1) * per, :]
        d = jnp.where(eye, dot(e, e, NT), 0.0)
        cols.append(jnp.sum(d, axis=1, keepdims=True))
        rows.append(jnp.sum(d, axis=0, keepdims=True))
    row_sq = jnp.concatenate(rows, axis=1)
    rate = 1.0 / (TEMPER * feat)
    degree = jnp.zeros((1, points), jnp.float32)
    step = 2 * per
    for i in range(points // step):
        g = dot(e_ref[i * step : (i + 1) * step, :], e_ref[...], NT)
        col_sq = jnp.concatenate(cols[2 * i : 2 * i + 2], axis=0)
        k = jnp.exp((2.0 * g - col_sq - row_sq) * rate)
        degree = degree + jnp.sum(k, axis=0, keepdims=True)
        k_ref[i * step : (i + 1) * step, :] = k.astype(jnp.bfloat16)
    scale = 1.0 / jnp.sqrt(degree)
    lane = lax.broadcasted_iota(jnp.int32, (vecs, 2 * vecs), 1)
    unit = (lane == lax.broadcasted_iota(jnp.int32, (vecs, 2 * vecs), 0) + vecs).astype(jnp.float32)
    scaled = (v_ref[...] * scale).astype(jnp.bfloat16)
    mixed = dot(scaled, k_ref[...]) * scale
    for sweep in range(ITERS):
        last = sweep == ITERS - 1
        for i, part in enumerate(split(mixed, 3)):
            m_ref[i * vecs : (i + 1) * vecs, :] = part
        p = dot(m_ref[...], m_ref[...], NT)
        p = p[:vecs] + p[vecs : 2 * vecs] + p[2 * vecs :]
        p = p[:, : 2 * vecs] + jnp.concatenate([p[:, 2 * vecs :], jnp.zeros((vecs, vecs), jnp.float32)], axis=1)
        p = p + pltpu.roll(p, vecs, 1)
        full = jnp.where(lane < vecs, p, unit)
        if not last:
            weighted = jnp.concatenate(split(mixed * scale, 2), axis=0)
            ahead = dot(weighted, k_ref[...])
            ahead = (ahead[:vecs] + ahead[vecs:]) * scale
        inv = jnp.concatenate(inverse_factor([full[8 * t : 8 * t + 8, :] for t in range(vecs // 8)]), axis=0)
        inv = jnp.where(lane < vecs, 0.0, inv)
        if not last:
            inv = inv + pltpu.roll(inv, vecs, 1)
            parts = jnp.concatenate(split(inv, 2), axis=0)
            mixed = dot(parts, jnp.concatenate(split(ahead, 2), axis=0))
            mixed = mixed[:vecs] + mixed[vecs:]
        else:
            mine = mixed[:, :per]
            vectors = lax.dot_general(inv, jnp.concatenate([mine, mine], axis=0), NN, preferred_element_type=jnp.float32, precision=HIGHEST)
            out_ref[...] = vectors.T[:own, :] * math.sqrt(points)


def exchange(x, rows, cols, partner):
    pairs = []
    for r in range(rows):
        for c in range(cols):
            r2, c2 = partner(r, c)
            pairs.append((r * cols + c, r2 * cols + c2))
    return lax.ppermute(x, ("row", "col"), pairs)


def replicated(embeddings, start_block, rows, cols):
    own, feat = embeddings.shape
    vecs = start_block.shape[0]
    send = functools.partial(exchange, rows=rows, cols=cols)
    mine = pl.pallas_call(
        functools.partial(pack_kernel, vecs, feat),
        out_shape=pltpu.VMEM((own, feat + 2 * vecs), jnp.bfloat16),
        in_specs=[pl.BlockSpec(memory_space=pltpu.VMEM)] * 2,
        out_specs=pl.BlockSpec(memory_space=pltpu.VMEM),
    )(embeddings, start_block.T)
    along_z = [send(mine, partner=lambda r, c, d=d: (r ^ (2 * d), c)) for d in (1, 2, 3)]
    a = jnp.concatenate([mine] + along_z, axis=0)
    b = send(a, partner=lambda r, c: (r, c ^ 2) if c & 1 else (r ^ 1, c))
    c_ = send(a, partner=lambda r, c: (r ^ 1, c) if c & 1 else (r, c ^ 2))
    d_ = send(b, partner=lambda r, c: (r ^ 1, c) if c & 1 else (r, c ^ 2))
    pieces = []
    for piece in (a, b, c_, d_):
        pieces += [piece, send(piece, partner=lambda r, c: (r, c ^ 1))]
    count, per = len(pieces), a.shape[0]
    points = count * per
    return pl.pallas_call(
        functools.partial(embed_kernel, count, own, vecs, feat),
        out_shape=jax.ShapeDtypeStruct((own, vecs), jnp.float32),
        in_specs=[pl.BlockSpec(memory_space=pltpu.VMEM)] * count,
        out_specs=pl.BlockSpec(memory_space=pltpu.VMEM),
        scratch_shapes=[
            pltpu.VMEM((points, feat), jnp.bfloat16),
            pltpu.VMEM((points, points), jnp.bfloat16),
            pltpu.VMEM((vecs, points), jnp.float32),
            pltpu.VMEM((3 * vecs, points), jnp.bfloat16),
        ],
        compiler_params=pltpu.CompilerParams(vmem_limit_bytes=40 * 1024 * 1024),
    )(*pieces).T


def kernel_block(left, left_sq, right):
    right_sq = jnp.sum(jnp.square(right.astype(jnp.float32)), axis=1)
    inner = lax.dot_general(left, right, NT, preferred_element_type=jnp.float32)
    return jnp.exp(-(left_sq[:, None] + right_sq[None, :] - 2.0 * inner) / (TEMPER * left.shape[1]))


def distributed(embeddings, start_block):
    per_device = embeddings.shape[0]
    total = lax.axis_size("row") * lax.axis_size("col") * per_device
    row_block = lax.all_gather(embeddings, "col", axis=0, tiled=True)
    row_sq = jnp.sum(jnp.square(row_block.astype(jnp.float32)), axis=1)
    vectors = start_block
    column_block = lax.all_gather(embeddings, "row", axis=0, tiled=True)
    degree_terms = jnp.sum(kernel_block(row_block, row_sq, column_block), axis=1)
    degree = lax.psum_scatter(degree_terms, "col", scatter_dimension=0, tiled=True)
    scale = 1.0 / jnp.sqrt(degree)
    for sweep in range(ITERS):
        scaled = (vectors * scale[None, :]).astype(jnp.bfloat16)
        column_vectors = lax.all_gather(scaled, "row", axis=1, tiled=True)
        tile = kernel_block(row_block, row_sq, column_block).astype(jnp.bfloat16)
        partial_rows = lax.dot_general(column_vectors, tile, NT, preferred_element_type=jnp.float32)
        mixed = lax.psum_scatter(partial_rows, "col", scatter_dimension=1, tiled=True) * scale[None, :]
        gram = lax.psum(jnp.dot(mixed, mixed.T, precision=HIGHEST), ("row", "col"))
        factor = jnp.linalg.cholesky(gram)
        vectors = jax.scipy.linalg.solve_triangular(factor, mixed, lower=True)
    return vectors * math.sqrt(total)


def solution(mesh):
    rows, cols = mesh.shape["row"], mesh.shape["col"]

    def body(embeddings, start_block):
        if (rows, cols) == (8, 4) and embeddings.shape[0] * 4 == 128 and start_block.shape[0] == 64:
            return replicated(embeddings, start_block, rows, cols)
        return distributed(embeddings, start_block)

    return jax.shard_map(
        body,
        mesh=mesh,
        in_specs=(P(("row", "col"), None), P(None, ("row", "col"))),
        out_specs=P(None, ("row", "col")),
        check_vma=False,
    )
```

```python
import functools
import math

import jax
import jax.numpy as jnp
from jax import lax
from jax.experimental import pallas as pl
from jax.experimental.pallas import tpu as pltpu
from jax.sharding import PartitionSpec as P

ITERS = 4
TEMPER = 0.5
HIGHEST = lax.Precision.HIGHEST
NT = (((1,), (1,)), ((), ()))
NN = (((1,), (0,)), ((), ()))


def lane_splat(x, c):
    return jnp.broadcast_to(x[:, c : c + 1], x.shape)


def row_splat(x, r):
    return jnp.broadcast_to(x[r : r + 1, :], x.shape)


def inverse_factor(tiles):
    count = len(tiles)
    sub = lax.broadcasted_iota(jnp.int32, tiles[0].shape, 0)
    pivots = [None] * count
    ahead = [lane_splat(tiles[0], j) for j in range(8)]
    for b in range(count):
        columns = [[ahead[j]] + [lane_splat(tiles[t], 8 * b + j) for t in range(b + 1, count)] for j in range(8)]
        if b + 1 < count:
            ahead = [lane_splat(tiles[b + 1], 8 * (b + 1) + j) for j in range(8)]
        factors, rows = [], []
        for j in range(8):
            pivot = row_splat(columns[j][0], j)
            q = pltpu.reciprocal(pivot, approx=True)
            m = [d * q for d in columns[j]]
            for l in range(j + 1, 8):
                head = row_splat(columns[l][0], j)
                columns[l] = [d - f * head for d, f in zip(columns[l], m)]
            if b + 1 < count:
                ahead = [d - m[1] * row_splat(columns[j][1], l) for l, d in enumerate(ahead)]
            row = row_splat(tiles[b], j)
            tiles[b] = tiles[b] - jnp.where(sub > j, m[0], 0.0) * row
            pivots[b] = pivot if j == 0 else jnp.where(sub >= j, pivot, pivots[b])
            factors.append(m)
            rows.append(row)
        for t in range(b + 1, count):
            total = factors[0][t - b] * rows[0]
            for j in range(1, 8):
                total = total + factors[j][t - b] * rows[j]
            tiles[t] = tiles[t] - total
    return [tile * lax.rsqrt(p) for tile, p in zip(tiles, pivots)]


def pack_kernel(vecs, feat, e_ref, s_ref, o_ref):
    o_ref[:, :feat] = e_ref[...]
    high = s_ref[...].astype(jnp.bfloat16)
    low = (s_ref[...] - high.astype(jnp.float32)).astype(jnp.bfloat16)
    o_ref[:, feat:] = jnp.concatenate([high, low], axis=1)


def split(x, parts):
    out = []
    for _ in range(parts - 1):
        out.append(x.astype(jnp.bfloat16))
        x = x - out[-1].astype(jnp.float32)
    return out + [x.astype(jnp.bfloat16)]


def dot(a, b, dims=NN):
    return lax.dot_general(a, b, dims, preferred_element_type=jnp.float32)


def embed_kernel(pieces, own, vecs, feat, *refs):
    piece_refs, out_ref = refs[:pieces], refs[pieces]
    e_ref, k_ref, x_ref, m_ref = refs[pieces + 1 :]
    points, per = e_ref.shape[0], 2 * vecs
    at = 0
    for piece in piece_refs:
        to = at + piece.shape[0]
        e_ref[at:to, :] = piece[:, :feat]
        x_ref[at:to, :] = piece[:, feat:].astype(jnp.float32)
        at = to
    eye = lax.broadcasted_iota(jnp.int32, (per, per), 0) == lax.broadcasted_iota(jnp.int32, (per, per), 1)
    cols, rows = [], []
    for i in range(points // per):
        e = e_ref[i * per : (i + 1) * per, :]
        d = jnp.where(eye, dot(e, e, NT), 0.0)
        cols.append(jnp.sum(d, axis=1, keepdims=True))
        rows.append(jnp.sum(d, axis=0, keepdims=True))
    row_sq = jnp.concatenate(rows, axis=1)
    rate = 1.0 / (TEMPER * feat)
    degree = jnp.zeros((1, points), jnp.float32)
    step = 2 * per
    for i in range(points // step):
        g = dot(e_ref[i * step : (i + 1) * step, :], e_ref[...], NT)
        col_sq = jnp.concatenate(cols[2 * i : 2 * i + 2], axis=0)
        k = jnp.exp((2.0 * g - col_sq - row_sq) * rate)
        degree = degree + jnp.sum(k, axis=0, keepdims=True)
        k_ref[i * step : (i + 1) * step, :] = k.astype(jnp.bfloat16)
    scale = 1.0 / jnp.sqrt(degree)
    lane = lax.broadcasted_iota(jnp.int32, (vecs, 2 * vecs), 1)
    unit = (lane == lax.broadcasted_iota(jnp.int32, (vecs, 2 * vecs), 0) + vecs).astype(jnp.float32)
    start = jnp.concatenate([x_ref[i * per : (i + 1) * per, :].T for i in range(points // per)], axis=1)
    scaled = ((start[:vecs] + start[vecs:]) * scale).astype(jnp.bfloat16)
    mixed = dot(scaled, k_ref[...]) * scale
    for sweep in range(ITERS):
        last = sweep == ITERS - 1
        for i, part in enumerate(split(mixed, 3)):
            m_ref[i * vecs : (i + 1) * vecs, :] = part
        p = dot(m_ref[...], m_ref[...], NT)
        p = p[:vecs] + p[vecs : 2 * vecs] + p[2 * vecs :]
        p = p[:, : 2 * vecs] + jnp.concatenate([p[:, 2 * vecs :], jnp.zeros((vecs, vecs), jnp.float32)], axis=1)
        p = p + pltpu.roll(p, vecs, 1)
        full = jnp.where(lane < vecs, p, unit)
        if not last:
            weighted = jnp.concatenate(split(mixed * scale, 2), axis=0)
            ahead = dot(weighted, k_ref[...])
            ahead = (ahead[:vecs] + ahead[vecs:]) * scale
        inv = jnp.concatenate(inverse_factor([full[8 * t : 8 * t + 8, :] for t in range(vecs // 8)]), axis=0)
        inv = jnp.where(lane < vecs, 0.0, inv)
        if not last:
            inv = inv + pltpu.roll(inv, vecs, 1)
            parts = jnp.concatenate(split(inv, 2), axis=0)
            mixed = dot(parts, jnp.concatenate(split(ahead, 2), axis=0))
            mixed = mixed[:vecs] + mixed[vecs:]
        else:
            mine = mixed[:, :per]
            vectors = lax.dot_general(inv, jnp.concatenate([mine, mine], axis=0), NN, preferred_element_type=jnp.float32, precision=HIGHEST)
            out_ref[...] = vectors.T[:own, :] * math.sqrt(points)


def exchange(x, rows, cols, partner):
    pairs = []
    for r in range(rows):
        for c in range(cols):
            r2, c2 = partner(r, c)
            pairs.append((r * cols + c, r2 * cols + c2))
    return lax.ppermute(x, ("row", "col"), pairs)


def replicated(embeddings, start_block, rows, cols):
    own, feat = embeddings.shape
    vecs = start_block.shape[0]
    send = functools.partial(exchange, rows=rows, cols=cols)
    mine = pl.pallas_call(
        functools.partial(pack_kernel, vecs, feat),
        out_shape=pltpu.VMEM((own, feat + 2 * vecs), jnp.bfloat16),
        in_specs=[pl.BlockSpec(memory_space=pltpu.VMEM)] * 2,
        out_specs=pl.BlockSpec(memory_space=pltpu.VMEM),
    )(embeddings, start_block.T)
    first = lambda r, c: (r, c ^ 2) if c & 1 else (r ^ 1, c)
    second = lambda r, c: (r ^ 1, c) if c & 1 else (r, c ^ 2)
    swap = lambda r, c: (r, c ^ 1)
    along_z = [send(mine, partner=lambda r, c, d=d: (r ^ (2 * d), c)) for d in (1, 2, 3)]
    px, py, pxy = (lambda r, c: (r, c ^ 2)), (lambda r, c: (r ^ 1, c)), (lambda r, c: (r ^ 1, c ^ 2))
    near = jnp.concatenate([mine, along_z[0]], axis=0)
    far = jnp.concatenate(along_z[1:], axis=0)
    pieces = [near, send(near, partner=swap), far, send(far, partner=swap)]
    for piece in (near, far):
        for p in (pxy, px, py):
            got = send(piece, partner=p)
            pieces += [got, send(got, partner=swap)]
    count = len(pieces)
    points = sum(piece.shape[0] for piece in pieces)
    return pl.pallas_call(
        functools.partial(embed_kernel, count, own, vecs, feat),
        out_shape=jax.ShapeDtypeStruct((own, vecs), jnp.float32),
        in_specs=[pl.BlockSpec(memory_space=pltpu.VMEM)] * count,
        out_specs=pl.BlockSpec(memory_space=pltpu.VMEM),
        scratch_shapes=[
            pltpu.VMEM((points, feat), jnp.bfloat16),
            pltpu.VMEM((points, points), jnp.bfloat16),
            pltpu.VMEM((points, 2 * vecs), jnp.float32),
            pltpu.VMEM((3 * vecs, points), jnp.bfloat16),
        ],
        compiler_params=pltpu.CompilerParams(vmem_limit_bytes=40 * 1024 * 1024),
    )(*pieces).T


def kernel_block(left, left_sq, right):
    right_sq = jnp.sum(jnp.square(right.astype(jnp.float32)), axis=1)
    inner = lax.dot_general(left, right, NT, preferred_element_type=jnp.float32)
    return jnp.exp(-(left_sq[:, None] + right_sq[None, :] - 2.0 * inner) / (TEMPER * left.shape[1]))


def distributed(embeddings, start_block):
    per_device = embeddings.shape[0]
    total = lax.axis_size("row") * lax.axis_size("col") * per_device
    row_block = lax.all_gather(embeddings, "col", axis=0, tiled=True)
    row_sq = jnp.sum(jnp.square(row_block.astype(jnp.float32)), axis=1)
    vectors = start_block
    column_block = lax.all_gather(embeddings, "row", axis=0, tiled=True)
    degree_terms = jnp.sum(kernel_block(row_block, row_sq, column_block), axis=1)
    degree = lax.psum_scatter(degree_terms, "col", scatter_dimension=0, tiled=True)
    scale = 1.0 / jnp.sqrt(degree)
    for sweep in range(ITERS):
        scaled = (vectors * scale[None, :]).astype(jnp.bfloat16)
        column_vectors = lax.all_gather(scaled, "row", axis=1, tiled=True)
        tile = kernel_block(row_block, row_sq, column_block).astype(jnp.bfloat16)
        partial_rows = lax.dot_general(column_vectors, tile, NT, preferred_element_type=jnp.float32)
        mixed = lax.psum_scatter(partial_rows, "col", scatter_dimension=1, tiled=True) * scale[None, :]
        gram = lax.psum(jnp.dot(mixed, mixed.T, precision=HIGHEST), ("row", "col"))
        factor = jnp.linalg.cholesky(gram)
        vectors = jax.scipy.linalg.solve_triangular(factor, mixed, lower=True)
    return vectors * math.sqrt(total)


def solution(mesh):
    rows, cols = mesh.shape["row"], mesh.shape["col"]

    def body(embeddings, start_block):
        if (rows, cols) == (8, 4) and embeddings.shape[0] * 4 == 128 and start_block.shape[0] == 64:
            return replicated(embeddings, start_block, rows, cols)
        return distributed(embeddings, start_block)

    return jax.shard_map(
        body,
        mesh=mesh,
        in_specs=(P(("row", "col"), None), P(None, ("row", "col"))),
        out_specs=P(None, ("row", "col")),
        check_vma=False,
    )
```

```python
import functools
import math

import jax
import jax.numpy as jnp
from jax import lax
from jax.experimental import pallas as pl
from jax.experimental.pallas import tpu as pltpu
from jax.sharding import PartitionSpec as P

ITERS = 4
TEMPER = 0.5
HIGHEST = lax.Precision.HIGHEST
NT = (((1,), (1,)), ((), ()))
NN = (((1,), (0,)), ((), ()))


def lane_splat(x, c):
    return jnp.broadcast_to(x[:, c : c + 1], x.shape)


def row_splat(x, r):
    return jnp.broadcast_to(x[r : r + 1, :], x.shape)


def inverse_factor(tiles):
    count = len(tiles)
    sub = lax.broadcasted_iota(jnp.int32, tiles[0].shape, 0)
    pivots = [None] * count
    ahead = [lane_splat(tiles[0], j) for j in range(8)]
    for b in range(count):
        columns = [[ahead[j]] + [lane_splat(tiles[t], 8 * b + j) for t in range(b + 1, count)] for j in range(8)]
        if b + 1 < count:
            ahead = [lane_splat(tiles[b + 1], 8 * (b + 1) + j) for j in range(8)]
        factors, rows = [], []
        for j in range(8):
            pivot = row_splat(columns[j][0], j)
            q = pltpu.reciprocal(pivot, approx=True)
            m = [d * q for d in columns[j]]
            for l in range(j + 1, 8):
                head = row_splat(columns[l][0], j)
                columns[l] = [d - f * head for d, f in zip(columns[l], m)]
            if b + 1 < count:
                ahead = [d - m[1] * row_splat(columns[j][1], l) for l, d in enumerate(ahead)]
            row = row_splat(tiles[b], j)
            tiles[b] = tiles[b] - jnp.where(sub > j, m[0], 0.0) * row
            pivots[b] = pivot if j == 0 else jnp.where(sub >= j, pivot, pivots[b])
            factors.append(m)
            rows.append(row)
        for t in range(b + 1, count):
            total = factors[0][t - b] * rows[0]
            for j in range(1, 8):
                total = total + factors[j][t - b] * rows[j]
            tiles[t] = tiles[t] - total
    return [tile * lax.rsqrt(p) for tile, p in zip(tiles, pivots)]


def pack_kernel(vecs, feat, e_ref, s_ref, o_ref):
    o_ref[:, :feat] = e_ref[...]
    high = s_ref[...].astype(jnp.bfloat16)
    low = (s_ref[...] - high.astype(jnp.float32)).astype(jnp.bfloat16)
    o_ref[:, feat:] = jnp.concatenate([high, low], axis=1)


def split(x, parts):
    out = []
    for _ in range(parts - 1):
        out.append(x.astype(jnp.bfloat16))
        x = x - out[-1].astype(jnp.float32)
    return out + [x.astype(jnp.bfloat16)]


def dot(a, b, dims=NN):
    return lax.dot_general(a, b, dims, preferred_element_type=jnp.float32)


def embed_kernel(pieces, own, vecs, feat, *refs):
    piece_refs, out_ref = refs[:pieces], refs[pieces]
    e_ref, k_ref, x_ref, m_ref = refs[pieces + 1 :]
    points, per = e_ref.shape[0], 2 * vecs
    at = 0
    for piece in piece_refs:
        to = at + piece.shape[0]
        e_ref[at:to, :] = piece[:, :feat]
        x_ref[at:to, :] = piece[:, feat:].astype(jnp.float32)
        at = to
    eye = lax.broadcasted_iota(jnp.int32, (per, per), 0) == lax.broadcasted_iota(jnp.int32, (per, per), 1)
    cols, rows = [], []
    for i in range(points // per):
        e = e_ref[i * per : (i + 1) * per, :]
        d = jnp.where(eye, dot(e, e, NT), 0.0)
        cols.append(jnp.sum(d, axis=1, keepdims=True))
        rows.append(jnp.sum(d, axis=0, keepdims=True))
    row_sq = jnp.concatenate(rows, axis=1)
    rate = 1.0 / (TEMPER * feat)
    degree = jnp.zeros((1, points), jnp.float32)
    step = 2 * per
    for i in range(points // step):
        g = dot(e_ref[i * step : (i + 1) * step, :], e_ref[...], NT)
        col_sq = jnp.concatenate(cols[2 * i : 2 * i + 2], axis=0)
        k = jnp.exp((2.0 * g - col_sq - row_sq) * rate)
        degree = degree + jnp.sum(k, axis=0, keepdims=True)
        k_ref[i * step : (i + 1) * step, :] = k.astype(jnp.bfloat16)
    scale = 1.0 / jnp.sqrt(degree)
    lane = lax.broadcasted_iota(jnp.int32, (vecs, 2 * vecs), 1)
    unit = (lane == lax.broadcasted_iota(jnp.int32, (vecs, 2 * vecs), 0) + vecs).astype(jnp.float32)
    start = jnp.concatenate([x_ref[i * per : (i + 1) * per, :].T for i in range(points // per)], axis=1)
    scaled = ((start[:vecs] + start[vecs:]) * scale).astype(jnp.bfloat16)
    mixed = dot(scaled, k_ref[...]) * scale
    for sweep in range(ITERS):
        last = sweep == ITERS - 1
        for i, part in enumerate(split(mixed, 3)):
            m_ref[i * vecs : (i + 1) * vecs, :] = part
        p = dot(m_ref[...], m_ref[...], NT)
        p = p[:vecs] + p[vecs : 2 * vecs] + p[2 * vecs :]
        p = p[:, : 2 * vecs] + jnp.concatenate([p[:, 2 * vecs :], jnp.zeros((vecs, vecs), jnp.float32)], axis=1)
        p = p + pltpu.roll(p, vecs, 1)
        full = jnp.where(lane < vecs, p, unit)
        if not last:
            weighted = jnp.concatenate(split(mixed * scale, 2), axis=0)
            ahead = dot(weighted, k_ref[...])
            ahead = (ahead[:vecs] + ahead[vecs:]) * scale
        inv = jnp.concatenate(inverse_factor([full[8 * t : 8 * t + 8, :] for t in range(vecs // 8)]), axis=0)
        inv = jnp.where(lane < vecs, 0.0, inv)
        if not last:
            inv = inv + pltpu.roll(inv, vecs, 1)
            parts = jnp.concatenate(split(inv, 2), axis=0)
            mixed = dot(parts, jnp.concatenate(split(ahead, 2), axis=0))
            mixed = mixed[:vecs] + mixed[vecs:]
        else:
            mine = mixed[:, :per]
            vectors = lax.dot_general(inv, jnp.concatenate([mine, mine], axis=0), NN, preferred_element_type=jnp.float32, precision=HIGHEST)
            out_ref[...] = vectors.T[:own, :] * math.sqrt(points)


def exchange(x, rows, cols, partner):
    pairs = []
    for r in range(rows):
        for c in range(cols):
            r2, c2 = partner(r, c)
            pairs.append((r * cols + c, r2 * cols + c2))
    return lax.ppermute(x, ("row", "col"), pairs)


def replicated(embeddings, start_block, rows, cols):
    own, feat = embeddings.shape
    vecs = start_block.shape[0]
    send = functools.partial(exchange, rows=rows, cols=cols)
    mine = pl.pallas_call(
        functools.partial(pack_kernel, vecs, feat),
        out_shape=pltpu.VMEM((own, feat + 2 * vecs), jnp.bfloat16),
        in_specs=[pl.BlockSpec(memory_space=pltpu.VMEM)] * 2,
        out_specs=pl.BlockSpec(memory_space=pltpu.VMEM),
    )(embeddings, start_block.T)
    along_x, along_y = (lambda r, c: (r, c ^ 2)), (lambda r, c: (r ^ 1, c))
    diagonal, swap = (lambda r, c: (r ^ 1, c ^ 2)), (lambda r, c: (r, c ^ 1))
    along_z = lambda d: lambda r, c: (r ^ (2 * d), c)
    farther = [send(mine, partner=along_z(d)) for d in (2, 3)]
    beside = send(mine, partner=along_z(1))
    own_x = send(mine, partner=along_x)
    own_y = send(mine, partner=along_y)
    own_d = send(mine, partner=diagonal)
    own_y, *farther = lax.optimization_barrier((own_y, *farther))
    far = jnp.concatenate(farther, axis=0)
    far_y = send(far, partner=along_y)
    far_d = send(far, partner=diagonal)
    far_x = send(far, partner=along_x)
    plane = jnp.concatenate([own_x, own_y, own_d], axis=0)
    beside_plane = send(plane, partner=along_z(1))
    near = jnp.concatenate([mine, plane], axis=0)
    pieces = []
    for piece in (near, beside, beside_plane, far, far_y, far_d, far_x):
        pieces += [piece, send(piece, partner=swap)]
    count = len(pieces)
    points = sum(piece.shape[0] for piece in pieces)
    return pl.pallas_call(
        functools.partial(embed_kernel, count, own, vecs, feat),
        out_shape=jax.ShapeDtypeStruct((own, vecs), jnp.float32),
        in_specs=[pl.BlockSpec(memory_space=pltpu.VMEM)] * count,
        out_specs=pl.BlockSpec(memory_space=pltpu.VMEM),
        scratch_shapes=[
            pltpu.VMEM((points, feat), jnp.bfloat16),
            pltpu.VMEM((points, points), jnp.bfloat16),
            pltpu.VMEM((points, 2 * vecs), jnp.float32),
            pltpu.VMEM((3 * vecs, points), jnp.bfloat16),
        ],
        compiler_params=pltpu.CompilerParams(vmem_limit_bytes=40 * 1024 * 1024),
    )(*pieces).T


def kernel_block(left, left_sq, right):
    right_sq = jnp.sum(jnp.square(right.astype(jnp.float32)), axis=1)
    inner = lax.dot_general(left, right, NT, preferred_element_type=jnp.float32)
    return jnp.exp(-(left_sq[:, None] + right_sq[None, :] - 2.0 * inner) / (TEMPER * left.shape[1]))


def distributed(embeddings, start_block):
    per_device = embeddings.shape[0]
    total = lax.axis_size("row") * lax.axis_size("col") * per_device
    row_block = lax.all_gather(embeddings, "col", axis=0, tiled=True)
    row_sq = jnp.sum(jnp.square(row_block.astype(jnp.float32)), axis=1)
    vectors = start_block
    column_block = lax.all_gather(embeddings, "row", axis=0, tiled=True)
    degree_terms = jnp.sum(kernel_block(row_block, row_sq, column_block), axis=1)
    degree = lax.psum_scatter(degree_terms, "col", scatter_dimension=0, tiled=True)
    scale = 1.0 / jnp.sqrt(degree)
    for sweep in range(ITERS):
        scaled = (vectors * scale[None, :]).astype(jnp.bfloat16)
        column_vectors = lax.all_gather(scaled, "row", axis=1, tiled=True)
        tile = kernel_block(row_block, row_sq, column_block).astype(jnp.bfloat16)
        partial_rows = lax.dot_general(column_vectors, tile, NT, preferred_element_type=jnp.float32)
        mixed = lax.psum_scatter(partial_rows, "col", scatter_dimension=1, tiled=True) * scale[None, :]
        gram = lax.psum(jnp.dot(mixed, mixed.T, precision=HIGHEST), ("row", "col"))
        factor = jnp.linalg.cholesky(gram)
        vectors = jax.scipy.linalg.solve_triangular(factor, mixed, lower=True)
    return vectors * math.sqrt(total)


def solution(mesh):
    rows, cols = mesh.shape["row"], mesh.shape["col"]

    def body(embeddings, start_block):
        if (rows, cols) == (8, 4) and embeddings.shape[0] * 4 == 128 and start_block.shape[0] == 64:
            return replicated(embeddings, start_block, rows, cols)
        return distributed(embeddings, start_block)

    return jax.shard_map(
        body,
        mesh=mesh,
        in_specs=(P(("row", "col"), None), P(None, ("row", "col"))),
        out_specs=P(None, ("row", "col")),
        check_vma=False,
    )
```

```python
import functools
import math

import jax
import jax.numpy as jnp
from jax import lax
from jax.experimental import pallas as pl
from jax.experimental.pallas import tpu as pltpu
from jax.sharding import PartitionSpec as P

ITERS = 4
TEMPER = 0.5
HIGHEST = lax.Precision.HIGHEST
NT = (((1,), (1,)), ((), ()))
NN = (((1,), (0,)), ((), ()))


def lane_splat(x, c):
    return jnp.broadcast_to(x[:, c : c + 1], x.shape)


def row_splat(x, r):
    return jnp.broadcast_to(x[r : r + 1, :], x.shape)


def inverse_factor(tiles):
    count = len(tiles)
    sub = lax.broadcasted_iota(jnp.int32, tiles[0].shape, 0)
    pivots = [None] * count
    ahead = [[lane_splat(tiles[k], j) for j in range(8)] for k in range(2)]
    for b in range(count):
        held = len(ahead)
        columns = [[a[j] for a in ahead] + [lane_splat(tiles[t], 8 * b + j) for t in range(b + held, count)] for j in range(8)]
        ahead = [[lane_splat(tiles[t], 8 * (b + 1) + j) for j in range(8)] for t in range(b + 1, min(b + 3, count))]
        factors, rows = [], []
        pivot = row_splat(columns[0][0], 0)
        for j in range(8):
            q = pltpu.reciprocal(pivot, approx=True)
            if j < 7:
                below = row_splat(columns[j][0], j + 1)
                coming = row_splat(columns[j + 1][0], j + 1) - below * below * q
            m = [d * q for d in columns[j]]
            for l in range(j + 1, 8):
                head = row_splat(columns[l][0], j)
                columns[l] = [d - f * head for d, f in zip(columns[l], m)]
            if ahead:
                heads = [row_splat(columns[j][1], l) for l in range(8)]
                ahead = [[d - m[1 + k] * h for d, h in zip(a, heads)] for k, a in enumerate(ahead)]
            row = row_splat(tiles[b], j)
            tiles[b] = tiles[b] - jnp.where(sub > j, m[0], 0.0) * row
            pivots[b] = pivot if j == 0 else jnp.where(sub >= j, pivot, pivots[b])
            if j < 7:
                pivot = coming
            factors.append(m)
            rows.append(row)
        for t in range(b + 1, count):
            total = factors[0][t - b] * rows[0]
            for j in range(1, 8):
                total = total + factors[j][t - b] * rows[j]
            tiles[t] = tiles[t] - total
    return [tile * lax.rsqrt(p) for tile, p in zip(tiles, pivots)]


def pack_kernel(vecs, feat, e_ref, s_ref, o_ref):
    o_ref[:, :feat] = e_ref[...]
    high = s_ref[...].astype(jnp.bfloat16)
    low = (s_ref[...] - high.astype(jnp.float32)).astype(jnp.bfloat16)
    o_ref[:, feat:] = jnp.concatenate([high, low], axis=1)


def split(x, parts):
    out = []
    for _ in range(parts - 1):
        out.append(x.astype(jnp.bfloat16))
        x = x - out[-1].astype(jnp.float32)
    return out + [x.astype(jnp.bfloat16)]


def dot(a, b, dims=NN):
    return lax.dot_general(a, b, dims, preferred_element_type=jnp.float32)


def embed_kernel(pieces, own, vecs, feat, *refs):
    piece_refs, out_ref = refs[:pieces], refs[pieces]
    e_ref, k_ref, x_ref, m_ref = refs[pieces + 1 :]
    points, per = e_ref.shape[0], 2 * vecs
    at = 0
    for piece in piece_refs:
        to = at + piece.shape[0]
        e_ref[at:to, :] = piece[:, :feat]
        x_ref[at:to, :] = piece[:, feat:].astype(jnp.float32)
        at = to
    eye = lax.broadcasted_iota(jnp.int32, (per, per), 0) == lax.broadcasted_iota(jnp.int32, (per, per), 1)
    cols, rows = [], []
    for i in range(points // per):
        e = e_ref[i * per : (i + 1) * per, :]
        d = jnp.where(eye, dot(e, e, NT), 0.0)
        cols.append(jnp.sum(d, axis=1, keepdims=True))
        rows.append(jnp.sum(d, axis=0, keepdims=True))
    row_sq = jnp.concatenate(rows, axis=1)
    rate = 1.0 / (TEMPER * feat)
    degree = jnp.zeros((1, points), jnp.float32)
    step = 2 * per
    for i in range(points // step):
        g = dot(e_ref[i * step : (i + 1) * step, :], e_ref[...], NT)
        col_sq = jnp.concatenate(cols[2 * i : 2 * i + 2], axis=0)
        k = jnp.exp((2.0 * g - col_sq - row_sq) * rate)
        degree = degree + jnp.sum(k, axis=0, keepdims=True)
        k_ref[i * step : (i + 1) * step, :] = k.astype(jnp.bfloat16)
    scale = 1.0 / jnp.sqrt(degree)
    lane = lax.broadcasted_iota(jnp.int32, (vecs, 2 * vecs), 1)
    unit = (lane == lax.broadcasted_iota(jnp.int32, (vecs, 2 * vecs), 0) + vecs).astype(jnp.float32)
    start = jnp.concatenate([x_ref[i * per : (i + 1) * per, :].T for i in range(points // per)], axis=1)
    scaled = ((start[:vecs] + start[vecs:]) * scale).astype(jnp.bfloat16)
    mixed = dot(scaled, k_ref[...]) * scale
    for sweep in range(ITERS):
        last = sweep == ITERS - 1
        for i, part in enumerate(split(mixed, 3)):
            m_ref[i * vecs : (i + 1) * vecs, :] = part
        p = dot(m_ref[...], m_ref[...], NT)
        p = p[:vecs] + p[vecs : 2 * vecs] + p[2 * vecs :]
        p = p[:, : 2 * vecs] + jnp.concatenate([p[:, 2 * vecs :], jnp.zeros((vecs, vecs), jnp.float32)], axis=1)
        p = p + pltpu.roll(p, vecs, 1)
        full = jnp.where(lane < vecs, p, unit)
        if not last:
            weighted = jnp.concatenate(split(mixed * scale, 2), axis=0)
            ahead = dot(weighted, k_ref[...])
            ahead = (ahead[:vecs] + ahead[vecs:]) * scale
        inv = jnp.concatenate(inverse_factor([full[8 * t : 8 * t + 8, :] for t in range(vecs // 8)]), axis=0)
        inv = jnp.where(lane < vecs, 0.0, inv)
        if not last:
            inv = inv + pltpu.roll(inv, vecs, 1)
            parts = jnp.concatenate(split(inv, 2), axis=0)
            mixed = dot(parts, jnp.concatenate(split(ahead, 2), axis=0))
            mixed = mixed[:vecs] + mixed[vecs:]
        else:
            mine = mixed[:, :per]
            vectors = lax.dot_general(inv, jnp.concatenate([mine, mine], axis=0), NN, preferred_element_type=jnp.float32, precision=HIGHEST)
            out_ref[...] = vectors.T[:own, :] * math.sqrt(points)


def exchange(x, rows, cols, partner):
    pairs = []
    for r in range(rows):
        for c in range(cols):
            r2, c2 = partner(r, c)
            pairs.append((r * cols + c, r2 * cols + c2))
    return lax.ppermute(x, ("row", "col"), pairs)


def replicated(embeddings, start_block, rows, cols):
    own, feat = embeddings.shape
    vecs = start_block.shape[0]
    send = functools.partial(exchange, rows=rows, cols=cols)
    mine = pl.pallas_call(
        functools.partial(pack_kernel, vecs, feat),
        out_shape=pltpu.VMEM((own, feat + 2 * vecs), jnp.bfloat16),
        in_specs=[pl.BlockSpec(memory_space=pltpu.VMEM)] * 2,
        out_specs=pl.BlockSpec(memory_space=pltpu.VMEM),
    )(embeddings, start_block.T)
    along_x, along_y = (lambda r, c: (r, c ^ 2)), (lambda r, c: (r ^ 1, c))
    diagonal, swap = (lambda r, c: (r ^ 1, c ^ 2)), (lambda r, c: (r, c ^ 1))
    along_z = lambda d: lambda r, c: (r ^ (2 * d), c)
    farther = [send(mine, partner=along_z(d)) for d in (2, 3)]
    beside = send(mine, partner=along_z(1))
    own_x = send(mine, partner=along_x)
    own_y = send(mine, partner=along_y)
    own_d = send(mine, partner=diagonal)
    own_y, *farther = lax.optimization_barrier((own_y, *farther))
    far = jnp.concatenate(farther, axis=0)
    far_y = send(far, partner=along_y)
    far_d = send(far, partner=diagonal)
    far_x = send(far, partner=along_x)
    plane = jnp.concatenate([own_x, own_y, own_d], axis=0)
    beside_plane = send(plane, partner=along_z(1))
    near = jnp.concatenate([mine, plane], axis=0)
    pieces = []
    for piece in (near, beside, beside_plane, far, far_y, far_d, far_x):
        pieces += [piece, send(piece, partner=swap)]
    count = len(pieces)
    points = sum(piece.shape[0] for piece in pieces)
    return pl.pallas_call(
        functools.partial(embed_kernel, count, own, vecs, feat),
        out_shape=jax.ShapeDtypeStruct((own, vecs), jnp.float32),
        in_specs=[pl.BlockSpec(memory_space=pltpu.VMEM)] * count,
        out_specs=pl.BlockSpec(memory_space=pltpu.VMEM),
        scratch_shapes=[
            pltpu.VMEM((points, feat), jnp.bfloat16),
            pltpu.VMEM((points, points), jnp.bfloat16),
            pltpu.VMEM((points, 2 * vecs), jnp.float32),
            pltpu.VMEM((3 * vecs, points), jnp.bfloat16),
        ],
        compiler_params=pltpu.CompilerParams(vmem_limit_bytes=40 * 1024 * 1024),
    )(*pieces).T


def kernel_block(left, left_sq, right):
    right_sq = jnp.sum(jnp.square(right.astype(jnp.float32)), axis=1)
    inner = lax.dot_general(left, right, NT, preferred_element_type=jnp.float32)
    return jnp.exp(-(left_sq[:, None] + right_sq[None, :] - 2.0 * inner) / (TEMPER * left.shape[1]))


def distributed(embeddings, start_block):
    per_device = embeddings.shape[0]
    total = lax.axis_size("row") * lax.axis_size("col") * per_device
    row_block = lax.all_gather(embeddings, "col", axis=0, tiled=True)
    row_sq = jnp.sum(jnp.square(row_block.astype(jnp.float32)), axis=1)
    vectors = start_block
    column_block = lax.all_gather(embeddings, "row", axis=0, tiled=True)
    degree_terms = jnp.sum(kernel_block(row_block, row_sq, column_block), axis=1)
    degree = lax.psum_scatter(degree_terms, "col", scatter_dimension=0, tiled=True)
    scale = 1.0 / jnp.sqrt(degree)
    for sweep in range(ITERS):
        scaled = (vectors * scale[None, :]).astype(jnp.bfloat16)
        column_vectors = lax.all_gather(scaled, "row", axis=1, tiled=True)
        tile = kernel_block(row_block, row_sq, column_block).astype(jnp.bfloat16)
        partial_rows = lax.dot_general(column_vectors, tile, NT, preferred_element_type=jnp.float32)
        mixed = lax.psum_scatter(partial_rows, "col", scatter_dimension=1, tiled=True) * scale[None, :]
        gram = lax.psum(jnp.dot(mixed, mixed.T, precision=HIGHEST), ("row", "col"))
        factor = jnp.linalg.cholesky(gram)
        vectors = jax.scipy.linalg.solve_triangular(factor, mixed, lower=True)
    return vectors * math.sqrt(total)


def solution(mesh):
    rows, cols = mesh.shape["row"], mesh.shape["col"]

    def body(embeddings, start_block):
        if (rows, cols) == (8, 4) and embeddings.shape[0] * 4 == 128 and start_block.shape[0] == 64:
            return replicated(embeddings, start_block, rows, cols)
        return distributed(embeddings, start_block)

    return jax.shard_map(
        body,
        mesh=mesh,
        in_specs=(P(("row", "col"), None), P(None, ("row", "col"))),
        out_specs=P(None, ("row", "col")),
        check_vma=False,
    )
```

```python
import functools
import math

import jax
import jax.numpy as jnp
from jax import lax
from jax.experimental import pallas as pl
from jax.experimental.pallas import tpu as pltpu
from jax.sharding import PartitionSpec as P

ITERS = 4
TEMPER = 0.5
HIGHEST = lax.Precision.HIGHEST
NT = (((1,), (1,)), ((), ()))
NN = (((1,), (0,)), ((), ()))


def lane_splat(x, c):
    return jnp.broadcast_to(x[:, c : c + 1], x.shape)


def row_splat(x, r):
    return jnp.broadcast_to(x[r : r + 1, :], x.shape)


def inverse_factor(tiles):
    count = len(tiles)
    sub = lax.broadcasted_iota(jnp.int32, tiles[0].shape, 0)
    pivots = [None] * count
    ahead = [[lane_splat(tiles[k], j) for j in range(8)] for k in range(2)]
    for b in range(count):
        held = len(ahead)
        columns = [[a[j] for a in ahead] + [lane_splat(tiles[t], 8 * b + j) for t in range(b + held, count)] for j in range(8)]
        ahead = [[lane_splat(tiles[t], 8 * (b + 1) + j) for j in range(8)] for t in range(b + 1, min(b + 3, count))]
        factors, rows = [], []
        pivot = row_splat(columns[0][0], 0)
        for j in range(8):
            q = pltpu.reciprocal(pivot, approx=True)
            if j < 7:
                below = row_splat(columns[j][0], j + 1)
                coming = row_splat(columns[j + 1][0], j + 1) - below * below * q
            m = [d * q for d in columns[j]]
            for l in range(j + 1, 8):
                head = row_splat(columns[l][0], j)
                columns[l] = [d - f * head for d, f in zip(columns[l], m)]
            if ahead:
                heads = [row_splat(columns[j][1], l) for l in range(8)]
                ahead = [[d - m[1 + k] * h for d, h in zip(a, heads)] for k, a in enumerate(ahead)]
            row = row_splat(tiles[b], j)
            tiles[b] = tiles[b] - jnp.where(sub > j, m[0], 0.0) * row
            pivots[b] = pivot if j == 0 else jnp.where(sub >= j, pivot, pivots[b])
            if j < 7:
                pivot = coming
            factors.append(m)
            rows.append(row)
        for t in range(b + 1, count):
            total = factors[0][t - b] * rows[0]
            for j in range(1, 8):
                total = total + factors[j][t - b] * rows[j]
            tiles[t] = tiles[t] - total
    return [tile * lax.rsqrt(p) for tile, p in zip(tiles, pivots)]


def pack_kernel(vecs, feat, e_ref, s_ref, o_ref):
    o_ref[:, :feat] = e_ref[...]
    high = s_ref[...].astype(jnp.bfloat16)
    low = (s_ref[...] - high.astype(jnp.float32)).astype(jnp.bfloat16)
    o_ref[:, feat:] = jnp.concatenate([high, low], axis=1)


def split(x, parts):
    out = []
    for _ in range(parts - 1):
        out.append(x.astype(jnp.bfloat16))
        x = x - out[-1].astype(jnp.float32)
    return out + [x.astype(jnp.bfloat16)]


def dot(a, b, dims=NN):
    return lax.dot_general(a, b, dims, preferred_element_type=jnp.float32)


def embed_kernel(pieces, own, vecs, feat, *refs):
    piece_refs, out_ref = refs[:pieces], refs[pieces]
    e_ref, k_ref, x_ref, m_ref = refs[pieces + 1 :]
    points, per = e_ref.shape[0], 2 * vecs
    at = 0
    for piece in piece_refs:
        to = at + piece.shape[0]
        e_ref[at:to, :] = piece[:, :feat]
        x_ref[at:to, :] = piece[:, feat:].astype(jnp.float32)
        at = to
    cols, rows = [], []
    for i in range(points // per):
        e = e_ref[i * per : (i + 1) * per, :].astype(jnp.float32)
        col = jnp.sum(e * e, axis=1, keepdims=True)
        cols.append(col)
        rows.append(jnp.broadcast_to(col, (per, per)).T[:1])
    row_sq = jnp.concatenate(rows, axis=1)
    rate = 1.0 / (TEMPER * feat)
    step = 2 * per
    blocks = points // step
    sums = [jnp.zeros((1, step), jnp.float32) for _ in range(blocks)]
    for i in range(blocks):
        lo, hi = i * step, (i + 1) * step
        g = dot(e_ref[lo:hi, :], e_ref[lo:, :], NT)
        col_sq = jnp.concatenate(cols[2 * i : 2 * i + 2], axis=0)
        k = jnp.exp((2.0 * g - col_sq - row_sq[:, lo:]) * rate)
        k_ref[lo:hi, lo:] = k.astype(jnp.bfloat16)
        for j in range(i, blocks):
            part = k[:, (j - i) * step : (j - i + 1) * step]
            sums[j] = sums[j] + jnp.sum(part, axis=0, keepdims=True)
            if j > i:
                part = part.T
                sums[i] = sums[i] + jnp.sum(part, axis=0, keepdims=True)
                k_ref[j * step : (j + 1) * step, lo:hi] = part.astype(jnp.bfloat16)
    degree = jnp.concatenate(sums, axis=1)
    scale = 1.0 / jnp.sqrt(degree)
    lane = lax.broadcasted_iota(jnp.int32, (vecs, 2 * vecs), 1)
    unit = (lane == lax.broadcasted_iota(jnp.int32, (vecs, 2 * vecs), 0) + vecs).astype(jnp.float32)
    start = jnp.concatenate([x_ref[i * per : (i + 1) * per, :].T for i in range(points // per)], axis=1)
    scaled = ((start[:vecs] + start[vecs:]) * scale).astype(jnp.bfloat16)
    mixed = dot(scaled, k_ref[...]) * scale
    for sweep in range(ITERS):
        last = sweep == ITERS - 1
        for i, part in enumerate(split(mixed, 3)):
            m_ref[i * vecs : (i + 1) * vecs, :] = part
        p = dot(m_ref[...], m_ref[...], NT)
        p = p[:vecs] + p[vecs : 2 * vecs] + p[2 * vecs :]
        p = p[:, : 2 * vecs] + jnp.concatenate([p[:, 2 * vecs :], jnp.zeros((vecs, vecs), jnp.float32)], axis=1)
        p = p + pltpu.roll(p, vecs, 1)
        full = jnp.where(lane < vecs, p, unit)
        if not last:
            weighted = jnp.concatenate(split(mixed * scale, 2), axis=0)
            ahead = dot(weighted, k_ref[...])
            ahead = (ahead[:vecs] + ahead[vecs:]) * scale
        inv = jnp.concatenate(inverse_factor([full[8 * t : 8 * t + 8, :] for t in range(vecs // 8)]), axis=0)
        inv = jnp.where(lane < vecs, 0.0, inv)
        if not last:
            inv = inv + pltpu.roll(inv, vecs, 1)
            parts = jnp.concatenate(split(inv, 2), axis=0)
            mixed = dot(parts, jnp.concatenate(split(ahead, 2), axis=0))
            mixed = mixed[:vecs] + mixed[vecs:]
        else:
            mine = mixed[:, :per]
            vectors = lax.dot_general(inv, jnp.concatenate([mine, mine], axis=0), NN, preferred_element_type=jnp.float32, precision=HIGHEST)
            out_ref[...] = vectors.T[:own, :] * math.sqrt(points)


def exchange(x, rows, cols, partner):
    pairs = []
    for r in range(rows):
        for c in range(cols):
            r2, c2 = partner(r, c)
            pairs.append((r * cols + c, r2 * cols + c2))
    return lax.ppermute(x, ("row", "col"), pairs)


def replicated(embeddings, start_block, rows, cols):
    own, feat = embeddings.shape
    vecs = start_block.shape[0]
    send = functools.partial(exchange, rows=rows, cols=cols)
    mine = pl.pallas_call(
        functools.partial(pack_kernel, vecs, feat),
        out_shape=pltpu.VMEM((own, feat + 2 * vecs), jnp.bfloat16),
        in_specs=[pl.BlockSpec(memory_space=pltpu.VMEM)] * 2,
        out_specs=pl.BlockSpec(memory_space=pltpu.VMEM),
    )(embeddings, start_block.T)
    along_x, along_y = (lambda r, c: (r, c ^ 2)), (lambda r, c: (r ^ 1, c))
    diagonal, swap = (lambda r, c: (r ^ 1, c ^ 2)), (lambda r, c: (r, c ^ 1))
    along_z = lambda d: lambda r, c: (r ^ (2 * d), c)
    farther = [send(mine, partner=along_z(d)) for d in (2, 3)]
    beside = send(mine, partner=along_z(1))
    own_x = send(mine, partner=along_x)
    own_y = send(mine, partner=along_y)
    own_d = send(mine, partner=diagonal)
    own_y, *farther = lax.optimization_barrier((own_y, *farther))
    far = jnp.concatenate(farther, axis=0)
    far_y = send(far, partner=along_y)
    far_d = send(far, partner=diagonal)
    far_x = send(far, partner=along_x)
    plane = jnp.concatenate([own_x, own_y, own_d], axis=0)
    beside_plane = send(plane, partner=along_z(1))
    near = jnp.concatenate([mine, plane], axis=0)
    pieces = []
    for piece in (near, beside, beside_plane, far, far_y, far_d, far_x):
        pieces += [piece, send(piece, partner=swap)]
    count = len(pieces)
    points = sum(piece.shape[0] for piece in pieces)
    return pl.pallas_call(
        functools.partial(embed_kernel, count, own, vecs, feat),
        out_shape=jax.ShapeDtypeStruct((own, vecs), jnp.float32),
        in_specs=[pl.BlockSpec(memory_space=pltpu.VMEM)] * count,
        out_specs=pl.BlockSpec(memory_space=pltpu.VMEM),
        scratch_shapes=[
            pltpu.VMEM((points, feat), jnp.bfloat16),
            pltpu.VMEM((points, points), jnp.bfloat16),
            pltpu.VMEM((points, 2 * vecs), jnp.float32),
            pltpu.VMEM((3 * vecs, points), jnp.bfloat16),
        ],
        compiler_params=pltpu.CompilerParams(vmem_limit_bytes=40 * 1024 * 1024),
    )(*pieces).T


def kernel_block(left, left_sq, right):
    right_sq = jnp.sum(jnp.square(right.astype(jnp.float32)), axis=1)
    inner = lax.dot_general(left, right, NT, preferred_element_type=jnp.float32)
    return jnp.exp(-(left_sq[:, None] + right_sq[None, :] - 2.0 * inner) / (TEMPER * left.shape[1]))


def distributed(embeddings, start_block):
    per_device = embeddings.shape[0]
    total = lax.axis_size("row") * lax.axis_size("col") * per_device
    row_block = lax.all_gather(embeddings, "col", axis=0, tiled=True)
    row_sq = jnp.sum(jnp.square(row_block.astype(jnp.float32)), axis=1)
    vectors = start_block
    column_block = lax.all_gather(embeddings, "row", axis=0, tiled=True)
    degree_terms = jnp.sum(kernel_block(row_block, row_sq, column_block), axis=1)
    degree = lax.psum_scatter(degree_terms, "col", scatter_dimension=0, tiled=True)
    scale = 1.0 / jnp.sqrt(degree)
    for sweep in range(ITERS):
        scaled = (vectors * scale[None, :]).astype(jnp.bfloat16)
        column_vectors = lax.all_gather(scaled, "row", axis=1, tiled=True)
        tile = kernel_block(row_block, row_sq, column_block).astype(jnp.bfloat16)
        partial_rows = lax.dot_general(column_vectors, tile, NT, preferred_element_type=jnp.float32)
        mixed = lax.psum_scatter(partial_rows, "col", scatter_dimension=1, tiled=True) * scale[None, :]
        gram = lax.psum(jnp.dot(mixed, mixed.T, precision=HIGHEST), ("row", "col"))
        factor = jnp.linalg.cholesky(gram)
        vectors = jax.scipy.linalg.solve_triangular(factor, mixed, lower=True)
    return vectors * math.sqrt(total)


def solution(mesh):
    rows, cols = mesh.shape["row"], mesh.shape["col"]

    def body(embeddings, start_block):
        if (rows, cols) == (8, 4) and embeddings.shape[0] * 4 == 128 and start_block.shape[0] == 64:
            return replicated(embeddings, start_block, rows, cols)
        return distributed(embeddings, start_block)

    return jax.shard_map(
        body,
        mesh=mesh,
        in_specs=(P(("row", "col"), None), P(None, ("row", "col"))),
        out_specs=P(None, ("row", "col")),
        check_vma=False,
    )
```

```python
import functools
import math

import jax
import jax.numpy as jnp
from jax import lax
from jax.experimental import pallas as pl
from jax.experimental.pallas import tpu as pltpu
from jax.sharding import PartitionSpec as P

ITERS = 4
TEMPER = 0.5
HIGHEST = lax.Precision.HIGHEST
NT = (((1,), (1,)), ((), ()))
NN = (((1,), (0,)), ((), ()))


def lane_splat(x, c):
    return jnp.broadcast_to(x[:, c : c + 1], x.shape)


def row_splat(x, r):
    return jnp.broadcast_to(x[r : r + 1, :], x.shape)


def inverse_factor(tiles):
    count = len(tiles)
    sub = lax.broadcasted_iota(jnp.int32, tiles[0].shape, 0)
    pivots = [None] * count
    ahead = [[lane_splat(tiles[k], j) for j in range(8)] for k in range(2)]
    for b in range(count):
        held = len(ahead)
        columns = [[a[j] for a in ahead] + [lane_splat(tiles[t], 8 * b + j) for t in range(b + held, count)] for j in range(8)]
        ahead = [[lane_splat(tiles[t], 8 * (b + 1) + j) for j in range(8)] for t in range(b + 1, min(b + 3, count))]
        factors, rows = [], []
        pivot = row_splat(columns[0][0], 0)
        for j in range(8):
            q = pltpu.reciprocal(pivot, approx=True)
            if j < 7:
                below = row_splat(columns[j][0], j + 1)
                coming = row_splat(columns[j + 1][0], j + 1) - below * below * q
            m = [d * q for d in columns[j]]
            for l in range(j + 1, 8):
                head = row_splat(columns[l][0], j)
                columns[l] = [d - f * head for d, f in zip(columns[l], m)]
            if ahead:
                heads = [row_splat(columns[j][1], l) for l in range(8)]
                ahead = [[d - m[1 + k] * h for d, h in zip(a, heads)] for k, a in enumerate(ahead)]
            row = row_splat(tiles[b], j)
            tiles[b] = tiles[b] - jnp.where(sub > j, m[0], 0.0) * row
            pivots[b] = pivot if j == 0 else jnp.where(sub >= j, pivot, pivots[b])
            if j < 7:
                pivot = coming
            factors.append(m)
            rows.append(row)
        for t in range(b + 1, count):
            total = factors[0][t - b] * rows[0]
            for j in range(1, 8):
                total = total + factors[j][t - b] * rows[j]
            tiles[t] = tiles[t] - total
    return [tile * lax.rsqrt(p) for tile, p in zip(tiles, pivots)]


def pack_kernel(vecs, feat, e_ref, s_ref, o_ref):
    o_ref[:, :feat] = e_ref[...]
    high = s_ref[...].astype(jnp.bfloat16)
    low = (s_ref[...] - high.astype(jnp.float32)).astype(jnp.bfloat16)
    o_ref[:, feat:] = jnp.concatenate([high, low], axis=1)


def split(x, parts):
    out = []
    for _ in range(parts - 1):
        out.append(x.astype(jnp.bfloat16))
        x = x - out[-1].astype(jnp.float32)
    return out + [x.astype(jnp.bfloat16)]


def dot(a, b, dims=NN):
    return lax.dot_general(a, b, dims, preferred_element_type=jnp.float32)


def embed_kernel(pieces, own, vecs, feat, *refs):
    piece_refs, out_ref = refs[:pieces], refs[pieces]
    e_ref, k_ref, x_ref, m_ref = refs[pieces + 1 :]
    points, per = e_ref.shape[0], 2 * vecs
    at = 0
    for piece in piece_refs:
        to = at + piece.shape[0]
        e_ref[at:to, :] = piece[:, :feat]
        x_ref[at:to, :] = piece[:, feat:].astype(jnp.float32)
        at = to
    cols, rows = [], []
    for i in range(points // per):
        e = e_ref[i * per : (i + 1) * per, :].astype(jnp.float32)
        col = jnp.sum(e * e, axis=1, keepdims=True) * (1.0 / (TEMPER * feat))
        cols.append(col)
        rows.append(jnp.broadcast_to(col, (per, per)).T[:1])
    row_sq = jnp.concatenate(rows, axis=1)
    rate = 1.0 / (TEMPER * feat)
    start = jnp.concatenate([x_ref[i * per : (i + 1) * per, :].T for i in range(points // per)], axis=1)
    start = start[:vecs] + start[vecs:]
    step = 2 * per
    blocks = points // step
    sums = [jnp.zeros((1, step), jnp.float32) for _ in range(blocks)]
    for i in range(blocks):
        lo, hi = i * step, (i + 1) * step
        g = dot(e_ref[lo:hi, :], e_ref[lo:, :], NT)
        col_sq = jnp.concatenate(cols[2 * i : 2 * i + 2], axis=0)
        k = jnp.exp(g * (2.0 * rate) - col_sq - row_sq[:, lo:])
        k_ref[lo:hi, lo:] = k.astype(jnp.bfloat16)
        for j in range(i, blocks):
            part = k[:, (j - i) * step : (j - i + 1) * step]
            sums[j] = sums[j] + jnp.sum(part, axis=0, keepdims=True)
            if j > i:
                part = part.T
                sums[i] = sums[i] + jnp.sum(part, axis=0, keepdims=True)
                k_ref[j * step : (j + 1) * step, lo:hi] = part.astype(jnp.bfloat16)
    degree = jnp.concatenate(sums, axis=1)
    scale = 1.0 / jnp.sqrt(degree)
    lane = lax.broadcasted_iota(jnp.int32, (vecs, 2 * vecs), 1)
    unit = (lane == lax.broadcasted_iota(jnp.int32, (vecs, 2 * vecs), 0) + vecs).astype(jnp.float32)
    scaled = (start * scale).astype(jnp.bfloat16)
    mixed = dot(scaled, k_ref[...]) * scale
    for sweep in range(ITERS):
        last = sweep == ITERS - 1
        for i, part in enumerate(split(mixed, 3)):
            m_ref[i * vecs : (i + 1) * vecs, :] = part
        p = dot(m_ref[...], m_ref[...], NT)
        p = p[:vecs] + p[vecs : 2 * vecs] + p[2 * vecs :]
        p = p[:, : 2 * vecs] + jnp.concatenate([p[:, 2 * vecs :], jnp.zeros((vecs, vecs), jnp.float32)], axis=1)
        p = p + pltpu.roll(p, vecs, 1)
        full = jnp.where(lane < vecs, p, unit)
        if not last:
            weighted = jnp.concatenate(split(mixed * scale, 2), axis=0)
            ahead = dot(weighted, k_ref[...])
            ahead = (ahead[:vecs] + ahead[vecs:]) * scale
        inv = jnp.concatenate(inverse_factor([full[8 * t : 8 * t + 8, :] for t in range(vecs // 8)]), axis=0)
        inv = jnp.where(lane < vecs, 0.0, inv)
        if not last:
            inv = inv + pltpu.roll(inv, vecs, 1)
            parts = jnp.concatenate(split(inv, 2), axis=0)
            mixed = dot(parts, jnp.concatenate(split(ahead, 2), axis=0))
            mixed = mixed[:vecs] + mixed[vecs:]
        else:
            mine = mixed[:, :per]
            vectors = lax.dot_general(inv, jnp.concatenate([mine, mine], axis=0), NN, preferred_element_type=jnp.float32, precision=HIGHEST)
            out_ref[...] = vectors.T[:own, :] * math.sqrt(points)


def exchange(x, rows, cols, partner):
    pairs = []
    for r in range(rows):
        for c in range(cols):
            r2, c2 = partner(r, c)
            pairs.append((r * cols + c, r2 * cols + c2))
    return lax.ppermute(x, ("row", "col"), pairs)


def replicated(embeddings, start_block, rows, cols):
    own, feat = embeddings.shape
    vecs = start_block.shape[0]
    send = functools.partial(exchange, rows=rows, cols=cols)
    mine = pl.pallas_call(
        functools.partial(pack_kernel, vecs, feat),
        out_shape=pltpu.VMEM((own, feat + 2 * vecs), jnp.bfloat16),
        in_specs=[pl.BlockSpec(memory_space=pltpu.VMEM)] * 2,
        out_specs=pl.BlockSpec(memory_space=pltpu.VMEM),
    )(embeddings, start_block.T)
    along_x, along_y = (lambda r, c: (r, c ^ 2)), (lambda r, c: (r ^ 1, c))
    diagonal, swap = (lambda r, c: (r ^ 1, c ^ 2)), (lambda r, c: (r, c ^ 1))
    along_z = lambda d: lambda r, c: (r ^ (2 * d), c)
    farther = [send(mine, partner=along_z(d)) for d in (2, 3)]
    beside = send(mine, partner=along_z(1))
    own_x = send(mine, partner=along_x)
    own_y = send(mine, partner=along_y)
    own_d = send(mine, partner=diagonal)
    own_y, *farther = lax.optimization_barrier((own_y, *farther))
    far = jnp.concatenate(farther, axis=0)
    far_y = send(far, partner=along_y)
    far_d = send(far, partner=diagonal)
    far_x = send(far, partner=along_x)
    plane = jnp.concatenate([own_x, own_y, own_d], axis=0)
    beside_plane = send(plane, partner=along_z(1))
    near = jnp.concatenate([mine, plane], axis=0)
    pieces = []
    for piece in (near, beside, beside_plane, far, far_y, far_d, far_x):
        pieces += [piece, send(piece, partner=swap)]
    count = len(pieces)
    points = sum(piece.shape[0] for piece in pieces)
    return pl.pallas_call(
        functools.partial(embed_kernel, count, own, vecs, feat),
        out_shape=jax.ShapeDtypeStruct((own, vecs), jnp.float32),
        in_specs=[pl.BlockSpec(memory_space=pltpu.VMEM)] * count,
        out_specs=pl.BlockSpec(memory_space=pltpu.VMEM),
        scratch_shapes=[
            pltpu.VMEM((points, feat), jnp.bfloat16),
            pltpu.VMEM((points, points), jnp.bfloat16),
            pltpu.VMEM((points, 2 * vecs), jnp.float32),
            pltpu.VMEM((3 * vecs, points), jnp.bfloat16),
        ],
        compiler_params=pltpu.CompilerParams(vmem_limit_bytes=40 * 1024 * 1024),
    )(*pieces).T


def kernel_block(left, left_sq, right):
    right_sq = jnp.sum(jnp.square(right.astype(jnp.float32)), axis=1)
    inner = lax.dot_general(left, right, NT, preferred_element_type=jnp.float32)
    return jnp.exp(-(left_sq[:, None] + right_sq[None, :] - 2.0 * inner) / (TEMPER * left.shape[1]))


def distributed(embeddings, start_block):
    per_device = embeddings.shape[0]
    total = lax.axis_size("row") * lax.axis_size("col") * per_device
    row_block = lax.all_gather(embeddings, "col", axis=0, tiled=True)
    row_sq = jnp.sum(jnp.square(row_block.astype(jnp.float32)), axis=1)
    vectors = start_block
    column_block = lax.all_gather(embeddings, "row", axis=0, tiled=True)
    degree_terms = jnp.sum(kernel_block(row_block, row_sq, column_block), axis=1)
    degree = lax.psum_scatter(degree_terms, "col", scatter_dimension=0, tiled=True)
    scale = 1.0 / jnp.sqrt(degree)
    for sweep in range(ITERS):
        scaled = (vectors * scale[None, :]).astype(jnp.bfloat16)
        column_vectors = lax.all_gather(scaled, "row", axis=1, tiled=True)
        tile = kernel_block(row_block, row_sq, column_block).astype(jnp.bfloat16)
        partial_rows = lax.dot_general(column_vectors, tile, NT, preferred_element_type=jnp.float32)
        mixed = lax.psum_scatter(partial_rows, "col", scatter_dimension=1, tiled=True) * scale[None, :]
        gram = lax.psum(jnp.dot(mixed, mixed.T, precision=HIGHEST), ("row", "col"))
        factor = jnp.linalg.cholesky(gram)
        vectors = jax.scipy.linalg.solve_triangular(factor, mixed, lower=True)
    return vectors * math.sqrt(total)


def solution(mesh):
    rows, cols = mesh.shape["row"], mesh.shape["col"]

    def body(embeddings, start_block):
        own, vecs = embeddings.shape[0], start_block.shape[0]
        if (rows, cols) == (8, 4) and own * cols == 2 * vecs == 128:
            return replicated(embeddings, start_block, rows, cols)
        return distributed(embeddings, start_block)

    return jax.shard_map(
        body,
        mesh=mesh,
        in_specs=(P(("row", "col"), None), P(None, ("row", "col"))),
        out_specs=P(None, ("row", "col")),
        check_vma=False,
    )
```

```python
import functools
import math

import jax
import jax.numpy as jnp
from jax import lax
from jax.experimental import pallas as pl
from jax.experimental.pallas import tpu as pltpu
from jax.sharding import PartitionSpec as P

ITERS = 4
TEMPER = 0.5
HIGHEST = lax.Precision.HIGHEST
NT = (((1,), (1,)), ((), ()))
NN = (((1,), (0,)), ((), ()))


def lane_splat(x, c):
    return jnp.broadcast_to(x[:, c : c + 1], x.shape)


def row_splat(x, r):
    return jnp.broadcast_to(x[r : r + 1, :], x.shape)


def inverse_factor(tiles):
    count = len(tiles)
    sub = lax.broadcasted_iota(jnp.int32, tiles[0].shape, 0)
    pivots = [None] * count
    ahead = [[lane_splat(tiles[k], j) for j in range(8)] for k in range(2)]
    for b in range(count):
        held = len(ahead)
        columns = [[a[j] for a in ahead] + [lane_splat(tiles[t], 8 * b + j) for t in range(b + held, count)] for j in range(8)]
        ahead = [[lane_splat(tiles[t], 8 * (b + 1) + j) for j in range(8)] for t in range(b + 1, min(b + 3, count))]
        factors, rows = [], []
        pivot = row_splat(columns[0][0], 0)
        for j in range(8):
            q = pltpu.reciprocal(pivot, approx=True)
            if j < 7:
                below = row_splat(columns[j][0], j + 1)
                coming = row_splat(columns[j + 1][0], j + 1) - below * below * q
            m = [d * q for d in columns[j]]
            for l in range(j + 1, 8):
                head = row_splat(columns[l][0], j)
                columns[l] = [d - f * head for d, f in zip(columns[l], m)]
            if ahead:
                heads = [row_splat(columns[j][1], l) for l in range(8)]
                ahead = [[d - m[1 + k] * h for d, h in zip(a, heads)] for k, a in enumerate(ahead)]
            row = row_splat(tiles[b], j)
            tiles[b] = tiles[b] - jnp.where(sub > j, m[0], 0.0) * row
            pivots[b] = pivot if j == 0 else jnp.where(sub >= j, pivot, pivots[b])
            if j < 7:
                pivot = coming
            factors.append(m)
            rows.append(row)
        for t in range(b + 1, count):
            total = factors[0][t - b] * rows[0]
            for j in range(1, 8):
                total = total + factors[j][t - b] * rows[j]
            tiles[t] = tiles[t] - total
    return [tile * lax.rsqrt(p) for tile, p in zip(tiles, pivots)]


def pack_kernel(vecs, feat, e_ref, s_ref, o_ref):
    o_ref[:, :feat] = e_ref[...]
    high = s_ref[...].astype(jnp.bfloat16)
    low = (s_ref[...] - high.astype(jnp.float32)).astype(jnp.bfloat16)
    o_ref[:, feat:] = jnp.concatenate([high, low], axis=1)


def split(x, parts):
    out = []
    for _ in range(parts - 1):
        out.append(x.astype(jnp.bfloat16))
        x = x - out[-1].astype(jnp.float32)
    return out + [x.astype(jnp.bfloat16)]


def dot(a, b, dims=NN):
    return lax.dot_general(a, b, dims, preferred_element_type=jnp.float32)


def embed_kernel(pieces, own, vecs, feat, *refs):
    piece_refs, out_ref = refs[:pieces], refs[pieces]
    e_ref, k_ref, x_ref = refs[pieces + 1 :]
    points, per = e_ref.shape[0], 2 * vecs
    at = 0
    for piece in piece_refs:
        to = at + piece.shape[0]
        e_ref[at:to, :] = piece[:, :feat]
        x_ref[at:to, :] = piece[:, feat:].astype(jnp.float32)
        at = to
    cols, rows = [], []
    for i in range(points // per):
        e = e_ref[i * per : (i + 1) * per, :].astype(jnp.float32)
        col = jnp.sum(e * e, axis=1, keepdims=True) * (1.0 / (TEMPER * feat))
        cols.append(col)
        rows.append(jnp.broadcast_to(col, (per, per)).T[:1])
    row_sq = jnp.concatenate(rows, axis=1)
    rate = 1.0 / (TEMPER * feat)
    start = jnp.concatenate([x_ref[i * per : (i + 1) * per, :].T for i in range(points // per)], axis=1)
    start = start[:vecs] + start[vecs:]
    step = 2 * per
    blocks = points // step
    sums = [jnp.zeros((1, step), jnp.float32) for _ in range(blocks)]
    for i in range(blocks):
        lo, hi = i * step, (i + 1) * step
        g = dot(e_ref[lo:hi, :], e_ref[lo:, :], NT)
        col_sq = jnp.concatenate(cols[2 * i : 2 * i + 2], axis=0)
        k = jnp.exp(g * (2.0 * rate) - col_sq - row_sq[:, lo:])
        k_ref[lo:hi, lo:] = k.astype(jnp.bfloat16)
        for j in range(i, blocks):
            part = k[:, (j - i) * step : (j - i + 1) * step]
            sums[j] = sums[j] + jnp.sum(part, axis=0, keepdims=True)
            if j > i:
                part = part.T
                sums[i] = sums[i] + jnp.sum(part, axis=0, keepdims=True)
                k_ref[j * step : (j + 1) * step, lo:hi] = part.astype(jnp.bfloat16)
    degree = jnp.concatenate(sums, axis=1)
    scale = 1.0 / jnp.sqrt(degree)
    lane = lax.broadcasted_iota(jnp.int32, (vecs, 2 * vecs), 1)
    unit = (lane == lax.broadcasted_iota(jnp.int32, (vecs, 2 * vecs), 0) + vecs).astype(jnp.float32)
    scaled = (start * scale).astype(jnp.bfloat16)
    mixed = dot(scaled, k_ref[...]) * scale
    for sweep in range(ITERS):
        last = sweep == ITERS - 1
        stack = jnp.concatenate(split(mixed, 3), axis=0)
        p = dot(stack, stack, NT)
        p = p[:vecs] + p[vecs : 2 * vecs] + p[2 * vecs :]
        p = p[:, : 2 * vecs] + jnp.concatenate([p[:, 2 * vecs :], jnp.zeros((vecs, vecs), jnp.float32)], axis=1)
        p = p + pltpu.roll(p, vecs, 1)
        full = jnp.where(lane < vecs, p, unit)
        if not last:
            weighted = jnp.concatenate(split(mixed * scale, 2), axis=0)
            ahead = dot(weighted, k_ref[...])
            ahead = (ahead[:vecs] + ahead[vecs:]) * scale
        inv = jnp.concatenate(inverse_factor([full[8 * t : 8 * t + 8, :] for t in range(vecs // 8)]), axis=0)
        inv = jnp.where(lane < vecs, 0.0, inv)
        if not last:
            inv = inv + pltpu.roll(inv, vecs, 1)
            parts = jnp.concatenate(split(inv, 2), axis=0)
            mixed = dot(parts, jnp.concatenate(split(ahead, 2), axis=0))
            mixed = mixed[:vecs] + mixed[vecs:]
        else:
            mine = mixed[:, :per]
            vectors = lax.dot_general(inv, jnp.concatenate([mine, mine], axis=0), NN, preferred_element_type=jnp.float32, precision=HIGHEST)
            out_ref[...] = vectors.T[:own, :] * math.sqrt(points)


def exchange(x, rows, cols, partner):
    pairs = []
    for r in range(rows):
        for c in range(cols):
            r2, c2 = partner(r, c)
            pairs.append((r * cols + c, r2 * cols + c2))
    return lax.ppermute(x, ("row", "col"), pairs)


def replicated(embeddings, start_block, rows, cols):
    own, feat = embeddings.shape
    vecs = start_block.shape[0]
    send = functools.partial(exchange, rows=rows, cols=cols)
    mine = pl.pallas_call(
        functools.partial(pack_kernel, vecs, feat),
        out_shape=pltpu.VMEM((own, feat + 2 * vecs), jnp.bfloat16),
        in_specs=[pl.BlockSpec(memory_space=pltpu.VMEM)] * 2,
        out_specs=pl.BlockSpec(memory_space=pltpu.VMEM),
    )(embeddings, start_block.T)
    along_x, along_y = (lambda r, c: (r, c ^ 2)), (lambda r, c: (r ^ 1, c))
    diagonal, swap = (lambda r, c: (r ^ 1, c ^ 2)), (lambda r, c: (r, c ^ 1))
    along_z = lambda d: lambda r, c: (r ^ (2 * d), c)
    farther = [send(mine, partner=along_z(d)) for d in (2, 3)]
    beside = send(mine, partner=along_z(1))
    own_x = send(mine, partner=along_x)
    own_y = send(mine, partner=along_y)
    own_d = send(mine, partner=diagonal)
    own_y, *farther = lax.optimization_barrier((own_y, *farther))
    far = jnp.concatenate(farther, axis=0)
    far_y = send(far, partner=along_y)
    far_d = send(far, partner=diagonal)
    far_x = send(far, partner=along_x)
    plane = jnp.concatenate([own_x, own_y, own_d], axis=0)
    beside_plane = send(plane, partner=along_z(1))
    near = jnp.concatenate([mine, plane], axis=0)
    pieces = []
    for piece in (near, beside, beside_plane, far, far_y, far_d, far_x):
        pieces += [piece, send(piece, partner=swap)]
    count = len(pieces)
    points = sum(piece.shape[0] for piece in pieces)
    return pl.pallas_call(
        functools.partial(embed_kernel, count, own, vecs, feat),
        out_shape=jax.ShapeDtypeStruct((own, vecs), jnp.float32),
        in_specs=[pl.BlockSpec(memory_space=pltpu.VMEM)] * count,
        out_specs=pl.BlockSpec(memory_space=pltpu.VMEM),
        scratch_shapes=[
            pltpu.VMEM((points, feat), jnp.bfloat16),
            pltpu.VMEM((points, points), jnp.bfloat16),
            pltpu.VMEM((points, 2 * vecs), jnp.float32),
        ],
        compiler_params=pltpu.CompilerParams(vmem_limit_bytes=40 * 1024 * 1024),
    )(*pieces).T


def kernel_block(left, left_sq, right):
    right_sq = jnp.sum(jnp.square(right.astype(jnp.float32)), axis=1)
    inner = lax.dot_general(left, right, NT, preferred_element_type=jnp.float32)
    return jnp.exp(-(left_sq[:, None] + right_sq[None, :] - 2.0 * inner) / (TEMPER * left.shape[1]))


def distributed(embeddings, start_block):
    per_device = embeddings.shape[0]
    total = lax.axis_size("row") * lax.axis_size("col") * per_device
    row_block = lax.all_gather(embeddings, "col", axis=0, tiled=True)
    row_sq = jnp.sum(jnp.square(row_block.astype(jnp.float32)), axis=1)
    vectors = start_block
    column_block = lax.all_gather(embeddings, "row", axis=0, tiled=True)
    degree_terms = jnp.sum(kernel_block(row_block, row_sq, column_block), axis=1)
    degree = lax.psum_scatter(degree_terms, "col", scatter_dimension=0, tiled=True)
    scale = 1.0 / jnp.sqrt(degree)
    for sweep in range(ITERS):
        scaled = (vectors * scale[None, :]).astype(jnp.bfloat16)
        column_vectors = lax.all_gather(scaled, "row", axis=1, tiled=True)
        tile = kernel_block(row_block, row_sq, column_block).astype(jnp.bfloat16)
        partial_rows = lax.dot_general(column_vectors, tile, NT, preferred_element_type=jnp.float32)
        mixed = lax.psum_scatter(partial_rows, "col", scatter_dimension=1, tiled=True) * scale[None, :]
        gram = lax.psum(jnp.dot(mixed, mixed.T, precision=HIGHEST), ("row", "col"))
        factor = jnp.linalg.cholesky(gram)
        vectors = jax.scipy.linalg.solve_triangular(factor, mixed, lower=True)
    return vectors * math.sqrt(total)


def solution(mesh):
    rows, cols = mesh.shape["row"], mesh.shape["col"]

    def body(embeddings, start_block):
        own, vecs = embeddings.shape[0], start_block.shape[0]
        if (rows, cols) == (8, 4) and own * cols == 2 * vecs == 128:
            return replicated(embeddings, start_block, rows, cols)
        return distributed(embeddings, start_block)

    return jax.shard_map(
        body,
        mesh=mesh,
        in_specs=(P(("row", "col"), None), P(None, ("row", "col"))),
        out_specs=P(None, ("row", "col")),
        check_vma=False,
    )
```
